128 devices in a mesh: face: 2 (over y_hi), tile: 64 (over x, z, y_lo, core).
Axes of the slice: x: 4, y: 4 (y_hi: 2, y_lo: 2; y = y_hi * 2 + y_lo), z: 4, core: 2. Of those that a mesh axis runs over, the one named last changes fastest.
Arguments:
- tracers: float32 [4, 32, 32, 8192], P(None, None, 'face', 'tile'), may hold values from -6 to 6
- wind_field: float32 [2, 32, 32, 8192], P(None, None, 'face', 'tile'), may hold values from -4 to 4
- metric: float32 [32, 8192], P('face', 'tile'), may hold values from 0.5 to 2
- forcing: bfloat16 [12, 44, 32, 8192], P(None, None, 'face', 'tile'), may hold values from -6 to 6
- aux_inputs: bfloat16 [384, 262144], P(None, ('face', 'tile')), may hold values from -6 to 6
- batch_pos: int32 [32, 8192], P('face', 'tile'), may hold values from 0 to 262143, as said below
- day_of_year: int32 [1], replicated, may hold values from 0 to 364
- w_in: bfloat16 [512, 556], replicated, may hold values from -0.25 to 0.25
- b_in: float32 [512], replicated, may hold values from -3 to 3
- w_mid: bfloat16 [512, 512], replicated, may hold values from -0.25 to 0.25
- b_mid: float32 [512], replicated, may hold values from -3 to 3
- w_out: bfloat16 [368, 512], replicated, may hold values from -0.25 to 0.25
- b_out: float32 [368], replicated, may hold values from -3 to 3
Outputs:
- updated: float32 [4, 32, 32, 8192], P(None, None, 'face', 'tile')
- diagnostics: bfloat16 [240, 262144], P(None, ('face', 'tile'))
The draws below stay inside these ranges and needn't reach their ends.
Inputs may be any that keep to these rules, and one draw needn't show every extreme that they name: batch_pos is a permutation of all column positions. Number the devices d = (face index) * 64 + (tile index), device d holding batch positions d * 2048 to (d + 1) * 2048 - 1 and a block of 2048 grid columns. Of the grid columns of device s, exactly 16 have batch positions in the block of each device d, namely d * 2048 + s * 16 + j for j from 0 to 15.
All inputs are finite; a program needn't handle non-finite values.
Results may differ from the reference program's by a relative error of at most 0.012.
Values may be sent and summed in bfloat16 or wider, within the bound.
A program may use at most 128 MiB of HBM per device.

```python
import math
import jax
import jax.numpy as jnp
import numpy as np
from jax import lax

LEV = 32
FIELDS = 4
SUBSTEPS = 4
MONTHS = 12
FORC = 44
IN = 556
HID = 512
OUT = 368
LX = 16
LY = 128
GX = 32
GY = 8192
COLS_DEV = 2048
COLS = 262144
CHAN = 128
AUX = 384
DIAG = 240
N_FACE = 2
N_TILE = 64


def draw_batch_pos(key, part):
    key = jax.random.fold_in(key, 7)
    devices = N_FACE * N_TILE
    columns = LX * LY
    per_peer = columns // devices
    keys = jax.random.split(key, devices)
    orders = jax.vmap(lambda single: jax.random.permutation(single, columns))(keys).astype(jnp.int32)
    rank = jnp.arange(columns, dtype=jnp.int32)
    source = jnp.arange(devices, dtype=jnp.int32)[:, None]
    values = (rank // per_peer)[None, :] * columns + source * per_peer + (rank % per_peer)[None, :]
    local = jnp.zeros((devices, columns), jnp.int32).at[source, orders].set(values)
    return local.reshape(N_FACE, N_TILE, LX, LY).transpose(0, 2, 1, 3).reshape(GX, GY)


def shard_levels(rng, shape, cuts, least, largest):
    factor_of, own = 1.0, jax.random.fold_in(rng, 6)
    for dim, blocks in cuts:
        steps = jnp.exp(jax.random.uniform(jax.random.fold_in(own, dim), (blocks,), jnp.float32, least / len(cuts), largest / len(cuts)))
        factor_of = factor_of * jnp.repeat(steps, shape[dim] // blocks).reshape([-1 if axis == dim else 1 for axis in range(len(shape))])
    return factor_of


def scatter_about(rng, dims, scale, reach, shards=(), kind=jnp.bfloat16):
    values = scale * jax.random.normal(rng, dims, jnp.float32)
    if shards:
        values = values * shard_levels(rng, dims, shards, -0.22, 0.18)
    return jnp.clip(values, -reach, reach).astype(kind)


def setup_inputs(seed: int = 0) -> dict:
    seeds = jax.random.split(jax.random.key(seed), 14)
    return {
        "tracers": scatter_about(seeds[0], (FIELDS, LEV, GX, GY), 1.0, 6.0, ((2, 2), (3, 64)), jnp.float32),
        "wind_field": scatter_about(seeds[1], (2, LEV, GX, GY), 1.0, 4.0, ((2, 2), (3, 64)), jnp.float32),
        "metric": jnp.clip(jnp.exp(math.log(2.0) - 1.3862944 * jax.random.uniform(seeds[2], (GX, GY), jnp.float32) ** shard_levels(seeds[2], (GX, GY), ((0, 2), (1, 64)), -0.2, 0.2)), 0.5, 2.0),
        "forcing": scatter_about(seeds[3], (MONTHS, FORC, GX, GY), 1.0, 6.0, ((2, 2), (3, 64))),
        "aux_inputs": scatter_about(seeds[4], (AUX, COLS), 1.0, 6.0, ((1, 128),)),
        "batch_pos": draw_batch_pos(jax.random.fold_in(seeds[13], 71), 0),
        "day_of_year": jax.random.randint(seeds[6], (1,), 0, 365).astype(jnp.int32),
        "w_in": scatter_about(seeds[7], (HID, IN), IN ** -0.5, 0.25),
        "b_in": scatter_about(seeds[8], (HID,), 0.5, 3.0, (), jnp.float32),
        "w_mid": scatter_about(seeds[9], (HID, HID), HID ** -0.5, 0.25),
        "b_mid": scatter_about(seeds[10], (HID,), 0.5, 3.0, (), jnp.float32),
        "w_out": scatter_about(seeds[11], (OUT, HID), HID ** -0.5, 0.25),
        "b_out": scatter_about(seeds[12], (OUT,), 0.5, 3.0, (), jnp.float32),
    }


leak_slope = 0.15
time_step = 0.05
physics_weight = 0.5

def gll_derivative():
    root = np.sqrt(5.0)
    big = 5.0 * (root + 1.0) / 4.0
    mid = 5.0 * (root - 1.0) / 4.0
    near = (root + 1.0) / 4.0
    far = (root - 1.0) / 4.0
    table = np.array([[-3.0, big, -mid, 0.5], [-near, 0.0, root / 2.0, -far], [far, -root / 2.0, 0.0, near], [-0.5, mid, -big, 3.0]])
    return table.astype(np.float32)

def gll_weights():
    return np.array([1.0 / 6.0, 5.0 / 6.0, 5.0 / 6.0, 1.0 / 6.0], dtype=np.float32)

def sum_copies(field):
    size_x = field.shape[-2]
    size_y = field.shape[-1]
    low_x = (jnp.arange(size_x) % 4 == 0).astype(jnp.float32)[:, None]
    high_x = (jnp.arange(size_x) % 4 == 3).astype(jnp.float32)[:, None]
    low_y = (jnp.arange(size_y) % 4 == 0).astype(jnp.float32)[None, :]
    high_y = (jnp.arange(size_y) % 4 == 3).astype(jnp.float32)[None, :]
    along_x = field + low_x * jnp.roll(field, 1, -2) + high_x * jnp.roll(field, -1, -2)
    return along_x + low_y * jnp.roll(along_x, 1, -1) + high_y * jnp.roll(along_x, -1, -1)

def leaky(value):
    return jnp.where(value > 0, value, leak_slope * value)

def column_model(block, w_in, b_in, w_mid, b_mid, w_out, b_out):
    hidden = jnp.dot(w_in, block, preferred_element_type=jnp.float32) + b_in[:, None]
    hidden = leaky(hidden).astype(jnp.bfloat16)
    hidden = jnp.dot(w_mid, hidden, preferred_element_type=jnp.float32) + b_mid[:, None]
    hidden = leaky(hidden).astype(jnp.bfloat16)
    result = jnp.dot(w_out, hidden, preferred_element_type=jnp.float32) + b_out[:, None]
    return result.astype(jnp.bfloat16)

def reference(tracers, wind_field, metric, forcing, aux_inputs, batch_pos, day_of_year, w_in, b_in, w_mid, b_mid, w_out, b_out):
    derivative = jnp.asarray(gll_derivative(), dtype=jnp.float32)
    weights = jnp.asarray(gll_weights(), dtype=jnp.float32)
    point_mass = metric * jnp.tile(weights, GX // 4)[:, None] * jnp.tile(weights, GY // 4)[None, :]
    inverse_mass = 1.0 / sum_copies(point_mass)
    state = tracers
    for step in range(SUBSTEPS):
        grad_x = jnp.einsum('ij,flejy->fleiy', derivative, state.reshape(FIELDS, LEV, GX // 4, 4, GY), precision=lax.Precision.HIGHEST).reshape(FIELDS, LEV, GX, GY)
        grad_y = jnp.einsum('ij,flxej->flxei', derivative, state.reshape(FIELDS, LEV, GX, GY // 4, 4), precision=lax.Precision.HIGHEST).reshape(FIELDS, LEV, GX, GY)
        tendency = -(wind_field[0][None] * grad_x + wind_field[1][None] * grad_y)
        state = state + time_step * sum_copies(point_mass * tendency) * inverse_mass
    columns = GX * GY
    dynamic = state.reshape(CHAN, columns).astype(jnp.bfloat16)
    month_lo = day_of_year[0] * 12 // 365
    fraction = (day_of_year[0] * 12 - month_lo * 365).astype(jnp.float32) / 365.0
    month_hi = (month_lo + 1) % 12
    lower = lax.dynamic_index_in_dim(forcing, month_lo, 0, keepdims=False).astype(jnp.float32)
    upper = lax.dynamic_index_in_dim(forcing, month_hi, 0, keepdims=False).astype(jnp.float32)
    forcing_now = ((1.0 - fraction) * lower + fraction * upper).reshape(FORC, columns).astype(jnp.bfloat16)
    position = batch_pos.reshape(columns)
    aux_here = jnp.take(aux_inputs, position, axis=1)
    inputs = jnp.concatenate([dynamic, forcing_now, aux_here], axis=0)
    blocks = inputs.reshape(IN, columns // COLS_DEV, COLS_DEV).transpose(1, 0, 2)
    outputs = lax.map(lambda block: column_model(block, w_in, b_in, w_mid, b_mid, w_out, b_out), blocks)
    outputs = outputs.transpose(1, 0, 2).reshape(OUT, columns)
    updated = state + physics_weight * outputs[:CHAN].astype(jnp.float32).reshape(FIELDS, LEV, GX, GY)
    diagnostics = jnp.zeros((DIAG, columns), jnp.bfloat16).at[:, position].set(outputs[CHAN:])
    return (updated, diagnostics)
```

```python
import functools

import jax
import jax.numpy as jnp
import numpy as np
from jax import lax
from jax.experimental import pallas as pl
from jax.experimental.pallas import tpu as pltpu
from jax.sharding import PartitionSpec as P

SUBSTEPS = 4
FIELDS = 4
LEVELS = 32
HALF = 16
SIZE_X = 16
SIZE_Y = 128
COLUMNS = SIZE_X * SIZE_Y
CHANNELS = FIELDS * LEVELS
FORC = 44
AUX = 384
HIDDEN = 512
OUT = 368
HALO = 16
WIDE = SIZE_Y + 2 * HALO
NODES = WIDE // 4
CHUNK = 256
TILE_GROUPS = 4

MESH = pl.DeviceIdType.MESH
leak_slope = 0.15
time_step = 0.05
physics_weight = 0.5

root = np.sqrt(5.0)
big = 5.0 * (root + 1.0) / 4.0
mid = 5.0 * (root - 1.0) / 4.0
near = (root + 1.0) / 4.0
far = (root - 1.0) / 4.0


def derivative(s):
    c, d = s[0] - s[3], s[1] - s[2]
    e = (s[1] + s[2]) - (s[0] + s[3])
    p = (-1.75) * c + ((big + mid) / 2.0) * d
    q = (-(near - far) / 2.0) * c - (root / 4.0) * d
    outer, inner = 1.25 * e, (root / 4.0) * e
    return [p + outer, q + inner, q - inner, p - outer]


def leaky(value):
    return jnp.where(value > 0, value, leak_slope * value)


def iota(shape, dim):
    return lax.broadcasted_iota(jnp.int32, shape, dim)


def dot(a, b, contract=((1,), (0,))):
    return lax.dot_general(a, b, (contract, ((), ())), preferred_element_type=jnp.float32)


NT = ((1,), (1,))
TN = ((0,), (0,))


def kernel(
    tiles,
    tracers,
    winds,
    metric,
    forcing,
    aux,
    batch_pos,
    day,
    w_in,
    b_in,
    w_mid,
    b_mid,
    w_out,
    b_out,
    updated,
    diagnostics,
    tracers_v,
    winds_v,
    metric_v,
    forcing_v,
    aux_v,
    w_in_v,
    w_mid_v,
    w_out_v,
    load_sem,
    half_f32,
    half_b16,
    wind_b16,
    state_in,
    wind_in,
    halo_state,
    halo_wind,
    metric_all,
    pos_all,
    state,
    wind,
    mass,
    inverse,
    rate,
    place,
    forc_rows,
    forc_mat,
    forc_out,
    forc_in,
    dyn,
    dyn_out,
    dyn_in,
    back_out,
    back_in,
    pre,
    w_aux,
    w_dyn,
    bias_in,
    bias_mid,
    bias_out,
    diag_v,
    total,
    updated_v,
    near_send,
    near_recv,
    halo_send,
    halo_recv,
    relay_send,
    forc_recv,
    dyn_recv,
    back_recv,
    out_sem,
):
    devices = 2 * tiles
    per_peer = COLUMNS // devices
    group = tiles // TILE_GROUPS
    f = lax.axis_index("face")
    t = lax.axis_index("tile")
    me = f * tiles + t
    u_me = t // group
    k_me = t % group
    right = lax.rem(t + 1, tiles)
    left = lax.rem(t + tiles - 1, tiles)
    other = 1 - f

    def at(p):
        return (p // tiles, lax.rem(p, tiles))

    def own_rows(p):
        return pl.ds(pl.multiple_of(p * per_peer, 16), per_peer)

    loads = [
        pltpu.make_async_copy(a, b, load_sem.at[i])
        for i, (a, b) in enumerate(
            (
                (winds, winds_v),
                (tracers, tracers_v),
                (metric, metric_v),
                (w_in, w_in_v),
                (aux, aux_v),
                (forcing, forcing_v),
                (w_mid, w_mid_v),
                (w_out, w_out_v),
            )
        )
    ]
    for load in loads:
        load.start()

    barrier = pltpu.get_barrier_semaphore()

    @pl.loop(1, devices)
    def _(k):
        p = lax.rem(me + k, devices)
        pl.semaphore_signal(barrier, inc=1, device_id=at(p), device_id_type=MESH)

    loads[0].wait()
    for h in range(2):
        for g in range(4):
            rows = [
                winds_v[pl.ds(c * 512 + h * 256 + xh * 8 + 2 * g + lo, HALF, stride=SIZE_X), :]
                for c in range(2)
                for lo in range(2)
                for xh in range(2)
            ]
            wind_b16[h, g] = jnp.concatenate(rows, axis=0).T.astype(jnp.bfloat16)
    loads[1].wait()
    for h in range(2):
        for x in range(8):
            rows = [
                tracers_v[pl.ds(i * 512 + h * 256 + xh * 8 + x, HALF, stride=SIZE_X), :]
                for xh in range(2)
                for i in range(FIELDS)
            ]
            turned = jnp.concatenate(rows, axis=0).T
            half_f32[h, x] = turned
            half_b16[h, x] = turned.astype(jnp.bfloat16)
    loads[2].wait()
    face_rows = pl.ds(pl.multiple_of(f * SIZE_X, SIZE_X), SIZE_X)
    metric_all[0, face_rows, :] = metric_v[...]
    pos_all[f] = batch_pos[...]

    pl.semaphore_wait(barrier, devices - 1)

    def remote(src, dst, send, recv, target):
        copy = pltpu.make_async_remote_copy(
            src, dst, send, recv, device_id=target, device_id_type=MESH
        )
        copy.start()
        return copy

    def arrived(ref, sem):
        pltpu.make_async_copy(ref, ref, sem).wait()

    partner = (other, t)
    sent = [
        remote(metric_v, metric_all.at[0, face_rows], near_send.at[0], near_recv.at[0], partner),
        remote(batch_pos, pos_all.at[f], near_send.at[1], near_recv.at[1], partner),
    ]
    sides = ((0, right, SIZE_Y - HALO), (1, left, 0))
    for face in range(2):
        for side, tile, start in sides:
            rows = pl.ds(start, HALO)
            for kind, src, dst in (
                (0, metric_v, metric_all.at[1 + side, face_rows]),
                (1, wind_b16.at[face, :, rows], halo_wind.at[side, f]),
                (2, half_b16.at[face, :, rows], halo_state.at[side, f]),
            ):
                sent.append(
                    remote(
                        src,
                        dst,
                        halo_send.at[kind, side, face],
                        halo_recv.at[kind, side, f],
                        (face, tile),
                    )
                )
    sent.append(remote(wind_b16.at[other], wind_in.at[f], near_send.at[2], near_recv.at[2], partner))
    sent.append(remote(half_b16.at[other], state_in.at[f], near_send.at[3], near_recv.at[3], partner))

    def fill_place(face):
        pos = pos_all[face]
        slot = pos // COLUMNS * per_peer + pos % per_peer

        @pl.loop(0, COLUMNS // CHUNK)
        def _(i):
            rows = pl.ds(pl.multiple_of(i * CHUNK, CHUNK), CHUNK)
            index = iota((CHUNK, SIZE_Y), 0)
            here = slot - i * CHUNK
            for x in range(SIZE_X):
                hit = index == here[x : x + 1, :]
                place[face, rows, x * SIZE_Y : (x + 1) * SIZE_Y] = hit.astype(jnp.bfloat16)

    fill_place(f)

    loads[5].wait()
    months = day[0] * 12
    month_lo = months // 365
    month_hi = lax.rem(month_lo + 1, 12)
    part = jnp.full((1, 1, SIZE_Y), months - month_lo * 365, jnp.int32).astype(jnp.float32) / 365.0
    for c in range(0, FORC, 4):
        lower = forcing_v[pl.ds(month_lo * FORC + c, 4)].astype(jnp.float32)
        upper = forcing_v[pl.ds(month_hi * FORC + c, 4)].astype(jnp.float32)
        now = (1.0 - part) * lower + part * upper
        forc_rows[c * SIZE_X : (c + 4) * SIZE_X, :] = now.reshape(4 * SIZE_X, SIZE_Y)
    forc_rows[FORC * SIZE_X :, :] = jnp.zeros((4 * SIZE_X, SIZE_Y), jnp.float32)
    forc_mat[48:, :] = jnp.zeros((80, COLUMNS), jnp.bfloat16)
    for x in range(SIZE_X):
        forc_mat[0:48, x * SIZE_Y : (x + 1) * SIZE_Y] = forc_rows[
            pl.ds(x, 48, stride=SIZE_X), :
        ].astype(jnp.bfloat16)

    def spread(first, out, dst, recv):
        @pl.loop(0, group)
        def _(k):
            p = first + lax.rem(k_me + k, group)

            @pl.when(p != me)
            def _():
                pltpu.make_async_remote_copy(
                    out.at[own_rows(p)],
                    dst.at[own_rows(me)],
                    relay_send,
                    recv,
                    device_id=at(p),
                    device_id_type=MESH,
                ).start()

            @pl.when(p == me)
            def _():
                pltpu.make_async_copy(out.at[own_rows(me)], dst.at[own_rows(me)], recv).start()

    @pl.loop(0, COLUMNS // CHUNK)
    def _(i):
        c = lax.rem(u_me + i, 2 * TILE_GROUPS)
        rows = pl.ds(pl.multiple_of(c * CHUNK, CHUNK), CHUNK)
        forc_out[rows, :] = dot(place[f, rows, :], forc_mat[...], NT).astype(jnp.bfloat16)
        spread(c * group, forc_out, forc_in, forc_recv)

    def spread_bias(ref, into, size):
        for k in range(0, size, 128):
            n = min(128, size - k)
            into[k : k + n, :] = jnp.broadcast_to(ref[:, k : k + n], (128, n)).T

    spread_bias(b_in, bias_in, HIDDEN)
    spread_bias(b_mid, bias_mid, HIDDEN)
    spread_bias(b_out, bias_out, OUT)
    loads[3].wait()
    w_aux[...] = w_in_v[:, CHANNELS + FORC :]
    lane = iota((CHANNELS, 512), 1)
    ch = (lane // 16) % 4 * LEVELS + lane // 128 % 2 * HALF + lane % 16
    pick = (iota((CHANNELS, 512), 0) == ch) & (lane // 64 % 2 == lane // 256)
    w_dyn[...] = dot(w_in_v[:, 0:CHANNELS], pick.astype(jnp.bfloat16)).astype(jnp.bfloat16)
    loads[4].wait()

    def twice(value):
        return jnp.concatenate([value, value], axis=1)

    @pl.loop(0, COLUMNS // CHUNK)
    def _(i):
        cols = pl.ds(pl.multiple_of(i * CHUNK, CHUNK), CHUNK)
        pre[:, cols] = dot(w_aux[...], aux_v[:, cols]) + twice(bias_in[...])

    arrived(metric_all.at[0, pl.ds(0, SIZE_X)], near_recv.at[0])
    for face in range(2):
        for side in range(2):
            arrived(metric_all.at[1 + side, pl.ds(0, SIZE_X)], halo_recv.at[0, side, face])

    def node_weight(shape, dim):
        n = iota(shape, dim) % 4
        return jnp.where((n == 0) | (n == 3), np.float32(1.0 / 6.0), np.float32(5.0 / 6.0))

    turned = []
    for k in range(3):
        block = metric_all[k] * node_weight((32, SIZE_Y), 0) * node_weight((32, SIZE_Y), 1)
        turned.append(jnp.concatenate([block] * 4, axis=0).T)
    points = jnp.concatenate([turned[0], turned[2][:HALO], turned[1][SIZE_Y - HALO :]], axis=0)
    node_x = iota((WIDE, 128), 1) % 4
    node_y = iota((WIDE, 128), 0) % 4
    along = points + jnp.where(node_x == 0, pltpu.roll(points, 1, 1), 0.0)
    along = along + jnp.where(node_x == 3, pltpu.roll(points, 127, 1), 0.0)
    both = along + jnp.where(node_y == 0, pltpu.roll(along, 1, 0), 0.0)
    both = both + jnp.where(node_y == 3, pltpu.roll(along, WIDE - 1, 0), 0.0)
    scaled, inverted = -time_step * points, 1.0 / both
    low = iota((WIDE, 128), 1) < 64
    for face in range(2):
        for x in range(8):
            k = face * SIZE_X + x
            for value, into in ((scaled, mass), (inverted, inverse)):
                one = jnp.broadcast_to(value[:, k : k + 1], (WIDE, 128))
                two = jnp.broadcast_to(value[:, k + 8 : k + 9], (WIDE, 128))
                into[face, x] = jnp.where(low, one, two)

    arrived(pos_all.at[0], near_recv.at[1])
    fill_place(other)

    wind_in[f] = wind_b16[f]
    state[f, :, 0:SIZE_Y, :] = half_f32[f]
    out_lane = iota((128, 512), 1)
    from_lane = out_lane // 128 * 32 + out_lane // 64 % 2 * 16 + out_lane % 16
    widen = (iota((128, 512), 0) == from_lane).astype(jnp.bfloat16)
    for kind in (1, 2):
        for face in range(2):
            for side in range(2):
                ref = (halo_wind, halo_state)[kind - 1].at[side, face]
                arrived(ref, halo_recv.at[kind, side, face])
    arrived(wind_in.at[0], near_recv.at[2])
    for face in range(2):
        for g in range(4):
            rows = jnp.concatenate(
                [wind_in[face, g], halo_wind[1, face, g], halo_wind[0, face, g]], axis=0
            )
            wide = dot(rows, widen)
            for c in range(2):
                for lo in range(2):
                    k = 2 * c + lo
                    x = 2 * g + lo
                    wind[c, face, x] = wide[:, k * 128 : (k + 1) * 128] * mass[face, x]
    for face in range(2):
        state[face, :, SIZE_Y : SIZE_Y + HALO, :] = halo_state[1, face].astype(jnp.float32)
        state[face, :, SIZE_Y + HALO :, :] = halo_state[0, face].astype(jnp.float32)
    arrived(state_in.at[0], near_recv.at[3])
    state[other, :, 0:SIZE_Y, :] = state_in[other].astype(jnp.float32)

    low_half = iota((NODES, 128), 1) < 64

    @pl.loop(0, SUBSTEPS)
    def _(step):
        @pl.loop(0, NODES // 8)
        def _(i):
            for face in range(2):
                for e in range(0, 8, 4):

                    def rows(j):
                        return pl.ds(i * 32 + j, 8, stride=4)

                    s = [[state[face, e + a, rows(j), :] for j in range(4)] for a in range(4)]
                    along_y = [derivative(s[a]) for a in range(4)]
                    for j in range(4):
                        along_x = derivative([s[a][j] for a in range(4)])
                        for a in range(4):
                            value = wind[0, face, e + a, rows(j), :] * along_x[a]
                            value = value + wind[1, face, e + a, rows(j), :] * along_y[a][j]
                            rate[face, e + a, j, pl.ds(pl.multiple_of(i * 8, 8), 8), :] = value

        def summed(face, x, j):
            value = rate[face, x, j]
            if x == 3:
                return value + rate[face, 4, j]
            if x == 4:
                return rate[face, 3, j] + value
            if x == 7:
                pair = jnp.where(low_half, rate[1 - face, 0, j], rate[face, 0, j])
                return value + pltpu.roll(pair, 64, 1)
            if x == 0:
                pair = jnp.where(low_half, rate[face, 7, j], rate[1 - face, 7, j])
                return value + pltpu.roll(pair, 64, 1)
            return value

        for face in range(2):
            for x in range(8):
                z = [summed(face, x, j) for j in range(4)]
                z[0], z[3] = (
                    z[0] + pltpu.roll(z[3], 1, 0),
                    z[3] + pltpu.roll(z[0], NODES - 1, 0),
                )
                for j in range(4):
                    rows = pl.ds(j, NODES, stride=4)
                    state[face, x, rows, :] = (
                        state[face, x, rows, :] + z[j] * inverse[face, x, rows, :]
                    )

    for face in range(2):
        for x in range(8):
            dyn[face, x * SIZE_Y : (x + 1) * SIZE_Y, :] = state[face, x, 0:SIZE_Y, :].astype(
                jnp.bfloat16
            )

    low_row = iota((CHUNK, 128), 1) < 64

    @pl.loop(0, 2 * TILE_GROUPS)
    def _(i):
        c = lax.rem(i, 2) * TILE_GROUPS + lax.rem(u_me + TILE_GROUPS - i // 2, TILE_GROUPS)
        rows = pl.ds(pl.multiple_of(c * CHUNK, CHUNK), CHUNK)
        q = [
            [dot(place[face, rows, xh * 1024 : (xh + 1) * 1024], dyn[face]) for xh in range(2)]
            for face in range(2)
        ]
        turn = pltpu.roll(jnp.where(low_row, q[1][0], q[0][1]), 64, 1)
        dyn_out[rows, :] = (jnp.where(low_row, q[0][0], q[1][1]) + turn).astype(jnp.bfloat16)
        spread(c * group, dyn_out, dyn_in, dyn_recv.at[f * TILE_GROUPS + u_me])

    arrived(forc_in, forc_recv)

    @pl.loop(0, COLUMNS // CHUNK)
    def _(i):
        cols = pl.ds(pl.multiple_of(i * CHUNK, CHUNK), CHUNK)
        pre[:, cols] += dot(w_in_v[:, CHANNELS : 2 * CHANNELS], forc_in[cols, :], NT)

    loads[6].wait()
    loads[7].wait()
    level_lane = iota((256, CHANNELS), 1)
    level_row = iota((256, CHANNELS), 0)

    @pl.loop(0, TILE_GROUPS)
    def _(v):
        u = lax.rem(u_me + v, TILE_GROUPS)
        halves = []
        for h in range(2):
            c = h * TILE_GROUPS + u
            rows = pl.ds(pl.multiple_of(c * CHUNK, CHUNK), CHUNK)
            arrived(dyn_in.at[rows], dyn_recv.at[c])
            halves.append(dyn_in[rows, :])
        block = jnp.concatenate(halves, axis=1)
        for face in range(2):
            c = face * TILE_GROUPS + u
            cols = pl.ds(pl.multiple_of(c * CHUNK, CHUNK), CHUNK)
            hidden = pre[:, cols] + dot(w_dyn[:, face * 256 : (face + 1) * 256], block, NT)
            hidden = leaky(hidden).astype(jnp.bfloat16)
            hidden = dot(w_mid_v[...], hidden) + twice(bias_mid[...])
            hidden = leaky(hidden).astype(jnp.bfloat16)
            result = dot(w_out_v[...], hidden) + twice(bias_out[...])
            result = result.astype(jnp.bfloat16)
            diag_v[:, cols] = result[CHANNELS:, :]
            row = level_lane // LEVELS * 16 + level_lane % 16
            row = row + level_lane // HALF % 2 * 128 + face * 64
            pick = (level_row == row).astype(jnp.bfloat16)
            change = result[0:CHANNELS, :].astype(jnp.float32).T
            value = dot(block, pick) + physics_weight * change
            back_out[cols, :] = value.astype(jnp.bfloat16)
            spread(c * group, back_out, back_in, back_recv.at[f * TILE_GROUPS + u_me])

    diag_copy = pltpu.make_async_copy(diag_v, diagnostics, out_sem.at[0])
    diag_copy.start()

    for v in range(TILE_GROUPS):
        u = lax.rem(u_me + TILE_GROUPS - v, TILE_GROUPS)
        for face in range(2):
            c = face * TILE_GROUPS + u
            rows = pl.ds(pl.multiple_of(c * CHUNK, CHUNK), CHUNK)
            arrived(back_in.at[rows], back_recv.at[c])
            back = back_in[rows, :]
            for k in range(0, COLUMNS, 512):
                value = dot(back, place[f, rows, k : k + 512], TN)
                if v == 0 and face == 0:
                    total[:, k : k + 512] = value
                elif v < TILE_GROUPS - 1 or face == 0:
                    total[:, k : k + 512] += value
                else:
                    value = total[:, k : k + 512] + value
                    for x in range(4):
                        updated_v[pl.ds(k // SIZE_Y + x, CHANNELS, stride=SIZE_X), :] = value[
                            :, x * SIZE_Y : (x + 1) * SIZE_Y
                        ]
    updated_copy = pltpu.make_async_copy(updated_v, updated, out_sem.at[1])
    updated_copy.start()
    for copy in sent:
        copy.wait_send()
    away = pl.ds(0, (devices - 1) * per_peer)
    for out in (forc_out, dyn_out, back_out):
        arrived(out.at[away], relay_send)
    diag_copy.wait()
    updated_copy.wait()


def local(
    tracers,
    wind_field,
    metric,
    forcing,
    aux_inputs,
    batch_pos,
    day_of_year,
    w_in,
    b_in,
    w_mid,
    b_mid,
    w_out,
    b_out,
):
    tiles = lax.axis_size("tile")
    anywhere = pl.BlockSpec(memory_space=pl.ANY)
    vmem = pl.BlockSpec(memory_space=pltpu.VMEM)
    f32, b16 = jnp.float32, jnp.bfloat16
    dma = pltpu.SemaphoreType.DMA
    scratch = [
        pltpu.VMEM((CHANNELS * SIZE_X, SIZE_Y), f32),
        pltpu.VMEM((2 * LEVELS * SIZE_X, SIZE_Y), f32),
        pltpu.VMEM((SIZE_X, SIZE_Y), f32),
        pltpu.VMEM((12 * FORC, SIZE_X, SIZE_Y), b16),
        pltpu.VMEM((AUX, COLUMNS), b16),
        pltpu.VMEM(w_in.shape, b16),
        pltpu.VMEM(w_mid.shape, b16),
        pltpu.VMEM(w_out.shape, b16),
        dma((8,)),
        pltpu.VMEM((2, 8, SIZE_Y, 128), f32),
        pltpu.VMEM((2, 8, SIZE_Y, 128), b16),
        pltpu.VMEM((2, 4, SIZE_Y, 128), b16),
        pltpu.VMEM((2, 8, SIZE_Y, 128), b16),
        pltpu.VMEM((2, 4, SIZE_Y, 128), b16),
        pltpu.VMEM((2, 2, 8, HALO, 128), b16),
        pltpu.VMEM((2, 2, 4, HALO, 128), b16),
        pltpu.VMEM((3, 2 * SIZE_X, SIZE_Y), f32),
        pltpu.VMEM((2, SIZE_X, SIZE_Y), jnp.int32),
        pltpu.VMEM((2, 8, WIDE, 128), f32),
        pltpu.VMEM((2, 2, 8, WIDE, 128), f32),
        pltpu.VMEM((2, 8, WIDE, 128), f32),
        pltpu.VMEM((2, 8, WIDE, 128), f32),
        pltpu.VMEM((2, 8, 4, NODES, 128), f32),
        pltpu.VMEM((2, COLUMNS, COLUMNS), b16),
        pltpu.VMEM((48 * SIZE_X, SIZE_Y), f32),
        pltpu.VMEM((128, COLUMNS), b16),
        pltpu.VMEM((COLUMNS, 128), b16),
        pltpu.VMEM((COLUMNS, 128), b16),
        pltpu.VMEM((2, COLUMNS // 2, 128), b16),
        pltpu.VMEM((COLUMNS, 128), b16),
        pltpu.VMEM((COLUMNS, 128), b16),
        pltpu.VMEM((COLUMNS, 128), b16),
        pltpu.VMEM((COLUMNS, 128), b16),
        pltpu.VMEM((HIDDEN, COLUMNS), f32),
        pltpu.VMEM((HIDDEN, AUX), b16),
        pltpu.VMEM((HIDDEN, 512), b16),
        pltpu.VMEM((HIDDEN, 128), f32),
        pltpu.VMEM((HIDDEN, 128), f32),
        pltpu.VMEM((OUT, 128), f32),
        pltpu.VMEM((OUT - CHANNELS, COLUMNS), b16),
        pltpu.VMEM((CHANNELS, COLUMNS), f32),
        pltpu.VMEM((CHANNELS * SIZE_X, SIZE_Y), f32),
        dma((4,)),
        dma((4,)),
        dma((3, 2, 2)),
        dma((3, 2, 2)),
        dma,
        dma,
        dma((2 * TILE_GROUPS,)),
        dma((2 * TILE_GROUPS,)),
        dma((2,)),
    ]
    updated, diagnostics = pl.pallas_call(
        functools.partial(kernel, tiles),
        out_shape=(
            jax.ShapeDtypeStruct((CHANNELS * SIZE_X, SIZE_Y), f32),
            jax.ShapeDtypeStruct((OUT - CHANNELS, COLUMNS), b16),
        ),
        in_specs=[
            anywhere,
            anywhere,
            anywhere,
            anywhere,
            anywhere,
            vmem,
            pl.BlockSpec(memory_space=pltpu.SMEM),
            anywhere,
            vmem,
            anywhere,
            vmem,
            anywhere,
            vmem,
        ],
        out_specs=(anywhere, anywhere),
        scratch_shapes=scratch,
        compiler_params=pltpu.CompilerParams(
            collective_id=0, has_side_effects=True, vmem_limit_bytes=60 * 2**20
        ),
    )(
        tracers.reshape(CHANNELS * SIZE_X, SIZE_Y),
        wind_field.reshape(2 * LEVELS * SIZE_X, SIZE_Y),
        metric,
        forcing.reshape(12 * FORC, SIZE_X, SIZE_Y),
        aux_inputs,
        batch_pos,
        day_of_year,
        w_in,
        b_in.reshape(1, HIDDEN),
        w_mid,
        b_mid.reshape(1, HIDDEN),
        w_out,
        b_out.reshape(1, OUT),
    )
    return updated.reshape(tracers.shape), diagnostics


def solution(mesh):
    placed = (
        P(None, None, "face", "tile"),
        P(None, None, "face", "tile"),
        P("face", "tile"),
        P(None, None, "face", "tile"),
        P(None, ("face", "tile")),
        P("face", "tile"),
        P(),
        P(),
        P(),
        P(),
        P(),
        P(),
        P(),
    )
    return jax.shard_map(
        local,
        mesh=mesh,
        in_specs=placed,
        out_specs=(P(None, None, "face", "tile"), P(None, ("face", "tile"))),
        check_vma=False,
    )
```

```python
import functools

import jax
import jax.numpy as jnp
import numpy as np
from jax import lax
from jax.experimental import pallas as pl
from jax.experimental.pallas import tpu as pltpu
from jax.sharding import PartitionSpec as P

SUBSTEPS = 4
FIELDS = 4
LEVELS = 32
HALF = 16
SIZE_X = 16
SIZE_Y = 128
COLUMNS = SIZE_X * SIZE_Y
CHANNELS = FIELDS * LEVELS
FORC = 44
AUX = 384
HIDDEN = 512
OUT = 368
HALO = 16
WIDE = SIZE_Y + 2 * HALO
NODES = WIDE // 4
CHUNK = 256
TILE_GROUPS = 4

MESH = pl.DeviceIdType.MESH
leak_slope = 0.15
time_step = 0.05
physics_weight = 0.5

root = np.sqrt(5.0)
big = 5.0 * (root + 1.0) / 4.0
mid = 5.0 * (root - 1.0) / 4.0
near = (root + 1.0) / 4.0
far = (root - 1.0) / 4.0


def derivative(s):
    c, d = s[0] - s[3], s[1] - s[2]
    e = (s[1] + s[2]) - (s[0] + s[3])
    p = (-1.75) * c + ((big + mid) / 2.0) * d
    q = (-(near - far) / 2.0) * c - (root / 4.0) * d
    outer, inner = 1.25 * e, (root / 4.0) * e
    return [p + outer, q + inner, q - inner, p - outer]


def leaky(value):
    return jnp.where(value > 0, value, leak_slope * value)


def iota(shape, dim):
    return lax.broadcasted_iota(jnp.int32, shape, dim)


def dot(a, b, contract=((1,), (0,))):
    return lax.dot_general(a, b, (contract, ((), ())), preferred_element_type=jnp.float32)


def stage(i):
    a = (i + 2) // 4
    pair = a % 2
    return 2 - a + pair * 2 * (i % 2), pair * ((i + 2) // 2 - 2) + (1 - pair) * (i % 2)


NT = ((1,), (1,))
TN = ((0,), (0,))


def kernel(
    tiles,
    tracers,
    winds,
    metric,
    forcing,
    aux,
    batch_pos,
    day,
    w_in,
    b_in,
    w_mid,
    b_mid,
    w_out,
    b_out,
    updated,
    diagnostics,
    tracers_v,
    winds_v,
    metric_v,
    forcing_v,
    aux_v,
    w_in_v,
    w_mid_v,
    w_out_v,
    load_sem,
    half_f32,
    half_b16,
    wind_b16,
    state_in,
    wind_in,
    halo_state,
    halo_wind,
    metric_all,
    pos_all,
    state,
    wind,
    mass,
    inverse,
    rate,
    place,
    forc_rows,
    forc_mat,
    forc_out,
    forc_in,
    dyn,
    dyn_out,
    dyn_in,
    back_out,
    back_in,
    pre,
    w_aux,
    w_forc,
    w_dyn,
    bias_in,
    bias_mid,
    bias_out,
    diag_v,
    total,
    near_send,
    near_recv,
    halo_send,
    halo_recv,
    relay_send,
    forc_send,
    forc_recv,
    dyn_recv,
    back_recv,
    out_sem,
):
    devices = 2 * tiles
    per_peer = COLUMNS // devices
    group = tiles // TILE_GROUPS
    f = lax.axis_index("face")
    t = lax.axis_index("tile")
    me = f * tiles + t
    u_me = t // group
    k_me = t % group
    right = lax.rem(t + 1, tiles)
    left = lax.rem(t + tiles - 1, tiles)
    other = 1 - f

    def at(p):
        return (p // tiles, lax.rem(p, tiles))

    def own_rows(p):
        return pl.ds(pl.multiple_of(p * per_peer, 16), per_peer)

    loads = [
        pltpu.make_async_copy(a, b, load_sem.at[i])
        for i, (a, b) in enumerate(
            (
                (winds, winds_v),
                (tracers, tracers_v),
                (metric, metric_v),
                (w_in, w_in_v),
                (aux, aux_v),
                (forcing, forcing_v),
                (w_mid, w_mid_v),
                (w_out, w_out_v),
            )
        )
    ]
    for load in loads:
        load.start()

    barrier = pltpu.get_barrier_semaphore()

    @pl.loop(1, devices)
    def _(k):
        p = lax.rem(me + k, devices)
        pl.semaphore_signal(barrier, inc=1, device_id=at(p), device_id_type=MESH)

    loads[0].wait()
    for h in range(2):
        for g in range(4):
            rows = [
                winds_v[pl.ds(c * 512 + h * 256 + xh * 8 + 2 * g + lo, HALF, stride=SIZE_X), :]
                for c in range(2)
                for lo in range(2)
                for xh in range(2)
            ]
            wind_b16[h, g] = jnp.concatenate(rows, axis=0).T.astype(jnp.bfloat16)
    loads[1].wait()
    for h in range(2):
        for x in range(8):
            rows = [
                tracers_v[pl.ds(i * 512 + h * 256 + xh * 8 + x, HALF, stride=SIZE_X), :]
                for xh in range(2)
                for i in range(FIELDS)
            ]
            turned = jnp.concatenate(rows, axis=0).T
            half_f32[h, x] = turned
            half_b16[h, x] = turned.astype(jnp.bfloat16)
    loads[2].wait()
    face_rows = pl.ds(pl.multiple_of(f * SIZE_X, SIZE_X), SIZE_X)
    metric_all[0, face_rows, :] = metric_v[...]
    pos_all[f] = batch_pos[...]

    pl.semaphore_wait(barrier, devices - 1)

    def remote(src, dst, send, recv, target):
        copy = pltpu.make_async_remote_copy(
            src, dst, send, recv, device_id=target, device_id_type=MESH
        )
        copy.start()
        return copy

    def arrived(ref, sem):
        pltpu.make_async_copy(ref, ref, sem).wait()

    partner = (other, t)
    sent = [
        remote(metric_v, metric_all.at[0, face_rows], near_send.at[0], near_recv.at[0], partner),
        remote(batch_pos, pos_all.at[f], near_send.at[1], near_recv.at[1], partner),
    ]
    sides = ((0, right, SIZE_Y - HALO), (1, left, 0))
    for face in range(2):
        for side, tile, start in sides:
            rows = pl.ds(start, HALO)
            for kind, src, dst in (
                (0, metric_v, metric_all.at[1 + side, face_rows]),
                (1, wind_b16.at[face, :, rows], halo_wind.at[side, f]),
                (2, half_b16.at[face, :, rows], halo_state.at[side, f]),
            ):
                sent.append(
                    remote(
                        src,
                        dst,
                        halo_send.at[kind, side, face],
                        halo_recv.at[kind, side, f],
                        (face, tile),
                    )
                )
    sent.append(remote(wind_b16.at[other], wind_in.at[f], near_send.at[2], near_recv.at[2], partner))
    sent.append(remote(half_b16.at[other], state_in.at[f], near_send.at[3], near_recv.at[3], partner))

    def fill_place(face):
        pos = pos_all[face]
        slot = pos // COLUMNS * per_peer + pos % per_peer

        @pl.loop(0, COLUMNS // CHUNK)
        def _(i):
            rows = pl.ds(pl.multiple_of(i * CHUNK, CHUNK), CHUNK)
            index = iota((CHUNK, SIZE_Y), 0)
            here = slot - i * CHUNK
            for x in range(SIZE_X):
                hit = index == here[x : x + 1, :]
                place[face, rows, x * SIZE_Y : (x + 1) * SIZE_Y] = hit.astype(jnp.bfloat16)

    fill_place(f)

    loads[5].wait()
    months = day[0] * 12
    month_lo = months // 365
    month_hi = lax.rem(month_lo + 1, 12)
    part = jnp.full((1, 1, SIZE_Y), months - month_lo * 365, jnp.int32).astype(jnp.float32) / 365.0
    for c in range(0, FORC, 4):
        lower = forcing_v[pl.ds(month_lo * FORC + c, 4)].astype(jnp.float32)
        upper = forcing_v[pl.ds(month_hi * FORC + c, 4)].astype(jnp.float32)
        now = (1.0 - part) * lower + part * upper
        forc_rows[c * SIZE_X : (c + 4) * SIZE_X, :] = now.reshape(4 * SIZE_X, SIZE_Y)
    forc_rows[FORC * SIZE_X :, :] = jnp.zeros((4 * SIZE_X, SIZE_Y), jnp.float32)
    for x in range(SIZE_X):
        block = forc_rows[pl.ds(x, 48, stride=SIZE_X), :].astype(jnp.bfloat16)
        for k in (0, 64):
            forc_mat[k : k + 48, x * SIZE_Y : (x + 1) * SIZE_Y] = block
    for k in (48, 112):
        forc_mat[k : k + 16, :] = jnp.zeros((16, COLUMNS), jnp.bfloat16)

    def spread(c, out, dst, recv):
        def send(k):
            p = c * group + lax.rem(k_me + k, group)
            pltpu.make_async_remote_copy(
                out.at[own_rows(p)],
                dst.at[own_rows(me)],
                relay_send,
                recv,
                device_id=at(p),
                device_id_type=MESH,
            ).start()

        own = c == f * TILE_GROUPS + u_me

        @pl.when(own)
        def _():
            for k in range(1, group):
                send(k)
            pltpu.make_async_copy(out.at[own_rows(me)], dst.at[own_rows(me)], recv).start()

        @pl.when(jnp.logical_not(own))
        def _():
            for k in range(group):
                send(k)

    chips = devices // 2
    core = lax.rem(t, 2)
    low_lane = iota((per_peer, 128), 1) < 64

    def chip_rows(g):
        return pl.ds(pl.multiple_of(g * per_peer, 16), per_peer)

    @pl.loop(0, COLUMNS // CHUNK)
    def _(i):
        n = CHUNK // per_peer
        rows = pl.ds(pl.multiple_of(i * CHUNK, CHUNK), CHUNK)
        value = dot(place[f, rows, :], forc_mat[...], NT)
        for k in range(0, max(n, 1), 2):
            both = [value[(k + m) * per_peer : (k + m + 1) * per_peer, :] for m in range(2)]
            packed = jnp.where(low_lane, both[0], both[1]).astype(jnp.bfloat16)
            forc_out[chip_rows((i * n + k) // 2), :] = packed

    chip = me // 2

    def send_forcing(k):
        g = lax.rem(chip + k, chips)
        pltpu.make_async_remote_copy(
            forc_out.at[chip_rows(g)],
            forc_in.at[core, chip_rows(chip)],
            forc_send.at[0],
            forc_recv.at[0],
            device_id=at(2 * g + core),
            device_id_type=MESH,
        ).start()

    def spread_bias(ref, into, size):
        for k in range(0, size, 128):
            n = min(128, size - k)
            into[k : k + n, :] = jnp.broadcast_to(ref[k : k + n].reshape(1, n), (128, n)).T

    spread_bias(b_in, bias_in, HIDDEN)
    spread_bias(b_mid, bias_mid, HIDDEN)
    spread_bias(b_out, bias_out, OUT)
    loads[3].wait()
    w_aux[...] = w_in_v[CHANNELS + FORC :, :].T
    row = iota((CHANNELS, 128), 0)
    pick = (iota((CHANNELS, 128), 1) == row + core * 64) & (row < FORC)
    w_forc[...] = dot(
        w_in_v[CHANNELS : 2 * CHANNELS, :], pick.astype(jnp.bfloat16), TN
    ).astype(jnp.bfloat16)
    lane = iota((CHANNELS, 512), 1)
    ch = (lane // 16) % 4 * LEVELS + lane // 128 % 2 * HALF + lane % 16
    pick = (iota((CHANNELS, 512), 0) == ch) & (lane // 64 % 2 == lane // 256)
    w_dyn[...] = dot(w_in_v[0:CHANNELS, :], pick.astype(jnp.bfloat16), TN).astype(jnp.bfloat16)
    loads[4].wait()

    def twice(value):
        return jnp.concatenate([value, value], axis=1)

    @pl.loop(0, COLUMNS // CHUNK)
    def _(i):
        cols = pl.ds(pl.multiple_of(i * CHUNK, CHUNK), CHUNK)
        pre[:, cols] = dot(w_aux[...], aux_v[:, cols]) + twice(bias_in[...])

    arrived(metric_all.at[0, pl.ds(0, SIZE_X)], near_recv.at[0])
    for face in range(2):
        for side in range(2):
            arrived(metric_all.at[1 + side, pl.ds(0, SIZE_X)], halo_recv.at[0, side, face])

    def node_weight(shape, dim):
        n = iota(shape, dim) % 4
        return jnp.where((n == 0) | (n == 3), np.float32(1.0 / 6.0), np.float32(5.0 / 6.0))

    turned = []
    for k in range(3):
        block = metric_all[k] * node_weight((32, SIZE_Y), 0) * node_weight((32, SIZE_Y), 1)
        turned.append(jnp.concatenate([block] * 4, axis=0).T)
    points = jnp.concatenate([turned[0], turned[2][:HALO], turned[1][SIZE_Y - HALO :]], axis=0)
    node_x = iota((WIDE, 128), 1) % 4
    node_y = iota((WIDE, 128), 0) % 4
    along = points + jnp.where(node_x == 0, pltpu.roll(points, 1, 1), 0.0)
    along = along + jnp.where(node_x == 3, pltpu.roll(points, 127, 1), 0.0)
    both = along + jnp.where(node_y == 0, pltpu.roll(along, 1, 0), 0.0)
    both = both + jnp.where(node_y == 3, pltpu.roll(along, WIDE - 1, 0), 0.0)
    scaled, inverted = -time_step * points, 1.0 / both
    low = iota((WIDE, 128), 1) < 64
    for face in range(2):
        for x in range(8):
            k = face * SIZE_X + x
            for value, into in ((scaled, mass), (inverted, inverse)):
                one = jnp.broadcast_to(value[:, k : k + 1], (WIDE, 128))
                two = jnp.broadcast_to(value[:, k + 8 : k + 9], (WIDE, 128))
                into[face, x] = jnp.where(low, one, two)

    arrived(pos_all.at[0], near_recv.at[1])
    fill_place(other)

    wind_in[f] = wind_b16[f]
    state[f, :, 0:SIZE_Y, :] = half_f32[f]
    out_lane = iota((128, 512), 1)
    from_lane = out_lane // 128 * 32 + out_lane // 64 % 2 * 16 + out_lane % 16
    widen = (iota((128, 512), 0) == from_lane).astype(jnp.bfloat16)
    for kind in (1, 2):
        for face in range(2):
            for side in range(2):
                ref = (halo_wind, halo_state)[kind - 1].at[side, face]
                arrived(ref, halo_recv.at[kind, side, face])
    arrived(wind_in.at[0], near_recv.at[2])
    for face in range(2):
        for g in range(4):
            rows = jnp.concatenate(
                [wind_in[face, g], halo_wind[1, face, g], halo_wind[0, face, g]], axis=0
            )
            wide = dot(rows, widen)
            for c in range(2):
                for lo in range(2):
                    k = 2 * c + lo
                    x = 2 * g + lo
                    wind[c, face, x] = wide[:, k * 128 : (k + 1) * 128] * mass[face, x]
    for face in range(2):
        state[face, :, SIZE_Y : SIZE_Y + HALO, :] = halo_state[1, face].astype(jnp.float32)
        state[face, :, SIZE_Y + HALO :, :] = halo_state[0, face].astype(jnp.float32)
    arrived(state_in.at[0], near_recv.at[3])
    state[other, :, 0:SIZE_Y, :] = state_in[other].astype(jnp.float32)

    low_half = iota((NODES, 128), 1) < 64

    @pl.loop(0, SUBSTEPS)
    def _(step):
        few = chips // SUBSTEPS
        for k in range(1, few):
            send_forcing(step * few + k)

        @pl.when(step > 0)
        def _():
            send_forcing(step * few)

        @pl.when(step == 0)
        def _():
            pltpu.make_async_copy(
                forc_out.at[chip_rows(chip)], forc_in.at[core, chip_rows(chip)], forc_recv.at[0]
            ).start()

        @pl.loop(0, NODES // 8)
        def _(i):
            for face in range(2):
                for e in range(0, 8, 4):

                    def rows(j):
                        return pl.ds(i * 32 + j, 8, stride=4)

                    s = [[state[face, e + a, rows(j), :] for j in range(4)] for a in range(4)]
                    along_y = [derivative(s[a]) for a in range(4)]
                    for j in range(4):
                        along_x = derivative([s[a][j] for a in range(4)])
                        for a in range(4):
                            value = wind[0, face, e + a, rows(j), :] * along_x[a]
                            value = value + wind[1, face, e + a, rows(j), :] * along_y[a][j]
                            rate[face, e + a, j, pl.ds(pl.multiple_of(i * 8, 8), 8), :] = value

        def summed(face, x, j):
            value = rate[face, x, j]
            if x == 3:
                return value + rate[face, 4, j]
            if x == 4:
                return rate[face, 3, j] + value
            if x == 7:
                pair = jnp.where(low_half, rate[1 - face, 0, j], rate[face, 0, j])
                return value + pltpu.roll(pair, 64, 1)
            if x == 0:
                pair = jnp.where(low_half, rate[face, 7, j], rate[1 - face, 7, j])
                return value + pltpu.roll(pair, 64, 1)
            return value

        for face in range(2):
            for x in range(8):
                z = [summed(face, x, j) for j in range(4)]
                z[0], z[3] = (
                    z[0] + pltpu.roll(z[3], 1, 0),
                    z[3] + pltpu.roll(z[0], NODES - 1, 0),
                )
                for j in range(4):
                    rows = pl.ds(j, NODES, stride=4)
                    state[face, x, rows, :] = (
                        state[face, x, rows, :] + z[j] * inverse[face, x, rows, :]
                    )

    for face in range(2):
        for x in range(8):
            dyn[face, x * SIZE_Y : (x + 1) * SIZE_Y, :] = state[face, x, 0:SIZE_Y, :].astype(
                jnp.bfloat16
            )

    low_row = iota((CHUNK, 128), 1) < 64

    @pl.loop(0, 2 * TILE_GROUPS)
    def _(i):
        on, face = stage(i)
        c = face * TILE_GROUPS + lax.rem(u_me + on, TILE_GROUPS)
        rows = pl.ds(pl.multiple_of(c * CHUNK, CHUNK), CHUNK)
        q = [
            [dot(place[face, rows, xh * 1024 : (xh + 1) * 1024], dyn[face]) for xh in range(2)]
            for face in range(2)
        ]
        turn = pltpu.roll(jnp.where(low_row, q[1][0], q[0][1]), 64, 1)
        dyn_out[rows, :] = (jnp.where(low_row, q[0][0], q[1][1]) + turn).astype(jnp.bfloat16)
        spread(c, dyn_out, dyn_in, dyn_recv.at[f * TILE_GROUPS + u_me])

    arrived(forc_in.at[core], forc_recv.at[0])
    sent.append(
        remote(
            forc_in.at[core],
            forc_in.at[core],
            forc_send.at[1],
            forc_recv.at[1],
            at(2 * chip + 1 - core),
        )
    )
    arrived(forc_in.at[1 - core], forc_recv.at[1])

    @pl.loop(0, COLUMNS // CHUNK)
    def _(i):
        cols = pl.ds(pl.multiple_of(i * CHUNK, CHUNK), CHUNK)
        half = CHUNK // 2
        blocks = []
        for k in range(0, half, per_peer):
            rows = pl.ds(pl.multiple_of(i * half + k, 16), per_peer)
            blocks += [forc_in[0, rows, :], forc_in[1, rows, :]]
        pre[:, cols] += dot(w_forc[...], jnp.concatenate(blocks, axis=0), NT)

    loads[6].wait()
    loads[7].wait()
    level_lane = iota((256, CHANNELS), 1)
    level_row = iota((256, CHANNELS), 0)

    @pl.loop(0, 2 * TILE_GROUPS)
    def _(i):
        on, face = stage(i)
        u = lax.rem(u_me + on, TILE_GROUPS)
        chunks = [
            pl.ds(pl.multiple_of((h * TILE_GROUPS + u) * CHUNK, CHUNK), CHUNK) for h in range(2)
        ]

        @pl.when((i == 0) | (i == 2) | (i == 3) | (i == 6))
        def _():
            for h in range(2):
                arrived(dyn_in.at[chunks[h]], dyn_recv.at[h * TILE_GROUPS + u])

        block = jnp.concatenate([dyn_in[chunks[0], :], dyn_in[chunks[1], :]], axis=1)
        c = face * TILE_GROUPS + u
        cols = pl.ds(pl.multiple_of(c * CHUNK, CHUNK), CHUNK)
        first = w_dyn[:, pl.ds(pl.multiple_of(face * 256, 256), 256)]
        hidden = leaky(pre[:, cols] + dot(first, block, NT)).astype(jnp.bfloat16)
        hidden = dot(w_mid_v[...], hidden) + twice(bias_mid[...])
        hidden = leaky(hidden).astype(jnp.bfloat16)
        result = dot(w_out_v[...], hidden) + twice(bias_out[...])
        result = result.astype(jnp.bfloat16)
        diag_v[:, cols] = result[CHANNELS:, :]
        row = level_lane // LEVELS * 16 + level_lane % 16
        row = row + level_lane // HALF % 2 * 128 + face * 64
        pick = (level_row == row).astype(jnp.bfloat16)
        change = result[0:CHANNELS, :].astype(jnp.float32).T
        value = dot(block, pick) + physics_weight * change
        back_out[cols, :] = value.astype(jnp.bfloat16)
        spread(c, back_out, back_in, back_recv.at[f * TILE_GROUPS + u_me])

    diag_copy = pltpu.make_async_copy(diag_v, diagnostics, out_sem.at[0])
    diag_copy.start()

    for v in (2, 1, 3, 0):
        u = lax.rem(u_me + TILE_GROUPS - v, TILE_GROUPS)
        parts = []
        for face in range(2):
            c = face * TILE_GROUPS + u
            rows = pl.ds(pl.multiple_of(c * CHUNK, CHUNK), CHUNK)
            arrived(back_in.at[rows], back_recv.at[c])
            parts.append((back_in[rows, :], rows))
        for k in range(0, COLUMNS, 512):
            value = sum(dot(back, place[f, rows, k : k + 512], TN) for back, rows in parts)
            value = value.astype(jnp.bfloat16)
            total[:, k : k + 512] = value if v == 2 else total[:, k : k + 512] + value
    updated_copy = pltpu.make_async_copy(total, updated, out_sem.at[1])
    updated_copy.start()
    for copy in sent:
        copy.wait_send()
    away = pl.ds(0, (devices - 1) * per_peer)
    for out in (dyn_out, back_out):
        arrived(out.at[away], relay_send)
    arrived(forc_out.at[pl.ds(0, (chips - 1) * per_peer)], forc_send.at[0])
    diag_copy.wait()
    updated_copy.wait()


PIECES = 4


def finish(new, diag, updated, diagnostics, new_v, diag_v, updated_v, load_sem, out_sem):
    n, d = CHANNELS // PIECES, (OUT - CHANNELS) // PIECES // 16 * 16
    cuts = [pl.ds(k * n, n) for k in range(PIECES)]
    cuts += [pl.ds(k * d, d if k < PIECES - 1 else OUT - CHANNELS - k * d) for k in range(PIECES)]
    ends = ((new, new_v),) * PIECES + ((diag, diag_v),) * PIECES
    loads = [
        pltpu.make_async_copy(src.at[cut], dst.at[cut], load_sem.at[k])
        for k, (cut, (src, dst)) in enumerate(zip(cuts, ends))
    ]
    for copy in loads:
        copy.start()
    outs = []

    def out(src, dst):
        outs.append(pltpu.make_async_copy(src, dst, out_sem.at[len(outs)]))
        outs[-1].start()

    for k in range(PIECES):
        loads[k].wait()
        for x in range(SIZE_X):
            block = new_v[k * n : (k + 1) * n, x * SIZE_Y : (x + 1) * SIZE_Y]
            updated_v[pl.ds(k * n * SIZE_X + x, n, stride=SIZE_X), :] = block.astype(jnp.float32)
        rows = pl.ds(k * n * SIZE_X, n * SIZE_X)
        out(updated_v.at[rows], updated.at[rows])
    for k in range(PIECES, 2 * PIECES):
        loads[k].wait()
        out(diag_v.at[cuts[k]], diagnostics.at[cuts[k]])
    for copy in outs:
        copy.wait()


def local(
    tracers,
    wind_field,
    metric,
    forcing,
    aux_inputs,
    batch_pos,
    day_of_year,
    w_in,
    b_in,
    w_mid,
    b_mid,
    w_out,
    b_out,
):
    tiles = lax.axis_size("tile")
    anywhere = pl.BlockSpec(memory_space=pl.ANY)
    vmem = pl.BlockSpec(memory_space=pltpu.VMEM)
    f32, b16 = jnp.float32, jnp.bfloat16
    dma = pltpu.SemaphoreType.DMA
    scratch = [
        pltpu.VMEM((CHANNELS * SIZE_X, SIZE_Y), f32),
        pltpu.VMEM((2 * LEVELS * SIZE_X, SIZE_Y), f32),
        pltpu.VMEM((SIZE_X, SIZE_Y), f32),
        pltpu.VMEM((12 * FORC, SIZE_X, SIZE_Y), b16),
        pltpu.VMEM((AUX, COLUMNS), b16),
        pltpu.VMEM(w_in.shape[::-1], b16),
        pltpu.VMEM(w_mid.shape, b16),
        pltpu.VMEM(w_out.shape, b16),
        dma((8,)),
        pltpu.VMEM((2, 8, SIZE_Y, 128), f32),
        pltpu.VMEM((2, 8, SIZE_Y, 128), b16),
        pltpu.VMEM((2, 4, SIZE_Y, 128), b16),
        pltpu.VMEM((2, 8, SIZE_Y, 128), b16),
        pltpu.VMEM((2, 4, SIZE_Y, 128), b16),
        pltpu.VMEM((2, 2, 8, HALO, 128), b16),
        pltpu.VMEM((2, 2, 4, HALO, 128), b16),
        pltpu.VMEM((3, 2 * SIZE_X, SIZE_Y), f32),
        pltpu.VMEM((2, SIZE_X, SIZE_Y), jnp.int32),
        pltpu.VMEM((2, 8, WIDE, 128), f32),
        pltpu.VMEM((2, 2, 8, WIDE, 128), f32),
        pltpu.VMEM((2, 8, WIDE, 128), f32),
        pltpu.VMEM((2, 8, WIDE, 128), f32),
        pltpu.VMEM((2, 8, 4, NODES, 128), f32),
        pltpu.VMEM((2, COLUMNS, COLUMNS), b16),
        pltpu.VMEM((48 * SIZE_X, SIZE_Y), f32),
        pltpu.VMEM((128, COLUMNS), b16),
        pltpu.VMEM((COLUMNS // 2, 128), b16),
        pltpu.VMEM((2, COLUMNS // 2, 128), b16),
        pltpu.VMEM((2, COLUMNS // 2, 128), b16),
        pltpu.VMEM((COLUMNS, 128), b16),
        pltpu.VMEM((COLUMNS, 128), b16),
        pltpu.VMEM((COLUMNS, 128), b16),
        pltpu.VMEM((COLUMNS, 128), b16),
        pltpu.VMEM((HIDDEN, COLUMNS), f32),
        pltpu.VMEM((HIDDEN, AUX), b16),
        pltpu.VMEM((HIDDEN, 128), b16),
        pltpu.VMEM((HIDDEN, 512), b16),
        pltpu.VMEM((HIDDEN, 128), f32),
        pltpu.VMEM((HIDDEN, 128), f32),
        pltpu.VMEM((OUT, 128), f32),
        pltpu.VMEM((OUT - CHANNELS, COLUMNS), b16),
        pltpu.VMEM((CHANNELS, COLUMNS), b16),
        dma((4,)),
        dma((4,)),
        dma((3, 2, 2)),
        dma((3, 2, 2)),
        dma,
        dma((2,)),
        dma((2,)),
        dma((2 * TILE_GROUPS,)),
        dma((2 * TILE_GROUPS,)),
        dma((2,)),
    ]
    updated, diagnostics = pl.pallas_call(
        functools.partial(kernel, tiles),
        out_shape=(
            jax.ShapeDtypeStruct((CHANNELS, COLUMNS), b16),
            jax.ShapeDtypeStruct((OUT - CHANNELS, COLUMNS), b16),
        ),
        in_specs=[
            anywhere,
            anywhere,
            anywhere,
            anywhere,
            anywhere,
            vmem,
            pl.BlockSpec(memory_space=pltpu.SMEM),
            anywhere,
            vmem,
            anywhere,
            vmem,
            anywhere,
            vmem,
        ],
        out_specs=(anywhere, anywhere),
        scratch_shapes=scratch,
        compiler_params=pltpu.CompilerParams(
            collective_id=0, has_side_effects=True, vmem_limit_bytes=60 * 2**20
        ),
    )(
        tracers.reshape(CHANNELS * SIZE_X, SIZE_Y),
        wind_field.reshape(2 * LEVELS * SIZE_X, SIZE_Y),
        metric,
        forcing.reshape(12 * FORC, SIZE_X, SIZE_Y),
        aux_inputs,
        batch_pos,
        day_of_year,
        w_in.T,
        b_in,
        w_mid,
        b_mid,
        w_out,
        b_out,
    )
    updated, diagnostics = pl.pallas_call(
        finish,
        out_shape=(
            jax.ShapeDtypeStruct((CHANNELS * SIZE_X, SIZE_Y), f32),
            jax.ShapeDtypeStruct((OUT - CHANNELS, COLUMNS), b16),
        ),
        in_specs=[anywhere, anywhere],
        out_specs=(anywhere, anywhere),
        scratch_shapes=[
            pltpu.VMEM((CHANNELS, COLUMNS), b16),
            pltpu.VMEM((OUT - CHANNELS, COLUMNS), b16),
            pltpu.VMEM((CHANNELS * SIZE_X, SIZE_Y), f32),
            dma((2 * PIECES,)),
            dma((2 * PIECES,)),
        ],
        compiler_params=pltpu.CompilerParams(vmem_limit_bytes=60 * 2**20),
    )(updated, diagnostics)
    return updated.reshape(tracers.shape), diagnostics


def solution(mesh):
    placed = (
        P(None, None, "face", "tile"),
        P(None, None, "face", "tile"),
        P("face", "tile"),
        P(None, None, "face", "tile"),
        P(None, ("face", "tile")),
        P("face", "tile"),
        P(),
        P(),
        P(),
        P(),
        P(),
        P(),
        P(),
    )
    return jax.shard_map(
        local,
        mesh=mesh,
        in_specs=placed,
        out_specs=(P(None, None, "face", "tile"), P(None, ("face", "tile"))),
        check_vma=False,
    )
```

```python
import functools

import jax
import jax.numpy as jnp
import numpy as np
from jax import lax
from jax.experimental import pallas as pl
from jax.experimental.pallas import tpu as pltpu
from jax.sharding import PartitionSpec as P

SUBSTEPS = 4
FIELDS = 4
LEVELS = 32
HALF = 16
SIZE_X = 16
SIZE_Y = 128
COLUMNS = SIZE_X * SIZE_Y
CHANNELS = FIELDS * LEVELS
FORC = 44
AUX = 384
HIDDEN = 512
OUT = 368
HALO = 16
WIDE = SIZE_Y + 2 * HALO
NODES = WIDE // 4
CHUNK = 256
TILE_GROUPS = 4

MESH = pl.DeviceIdType.MESH
leak_slope = 0.15
time_step = 0.05
physics_weight = 0.5

root = np.sqrt(5.0)
big = 5.0 * (root + 1.0) / 4.0
mid = 5.0 * (root - 1.0) / 4.0
near = (root + 1.0) / 4.0
far = (root - 1.0) / 4.0


def derivative(s):
    c, d = s[0] - s[3], s[1] - s[2]
    e = (s[1] + s[2]) - (s[0] + s[3])
    p = (-1.75) * c + ((big + mid) / 2.0) * d
    q = (-(near - far) / 2.0) * c - (root / 4.0) * d
    outer, inner = 1.25 * e, (root / 4.0) * e
    return [p + outer, q + inner, q - inner, p - outer]


def leaky(value):
    return jnp.where(value > 0, value, leak_slope * value)


def iota(shape, dim):
    return lax.broadcasted_iota(jnp.int32, shape, dim)


def dot(a, b, contract=((1,), (0,))):
    return lax.dot_general(a, b, (contract, ((), ())), preferred_element_type=jnp.float32)


def stage(i):
    return 2 - i + i // 2 * (7 - 2 * i)


NT = ((1,), (1,))
TN = ((0,), (0,))


def kernel(
    tiles,
    tracers,
    winds,
    metric,
    forcing,
    aux,
    batch_pos,
    day,
    w_in,
    b_in,
    w_mid,
    b_mid,
    w_out,
    b_out,
    updated,
    diagnostics,
    tracers_v,
    winds_v,
    metric_v,
    forcing_v,
    aux_v,
    w_in_v,
    w_mid_v,
    w_out_v,
    load_sem,
    half_b16,
    wind_b16,
    state_in,
    wind_in,
    halo_state,
    halo_wind,
    metric_all,
    pos_all,
    state,
    wind,
    mass,
    inverse,
    rate,
    place,
    forc_rows,
    forc_mat,
    forc_out,
    forc_in,
    dyn,
    dyn_out,
    dyn_in,
    back_out,
    back_in,
    pre,
    w_aux,
    w_forc,
    w_dyn,
    bias_in,
    bias_mid,
    bias_out,
    diag_v,
    total,
    known,
    near_send,
    near_recv,
    halo_send,
    halo_recv,
    relay_send,
    forc_send,
    forc_recv,
    dyn_recv,
    back_recv,
    out_sem,
):
    devices = 2 * tiles
    per_peer = COLUMNS // devices
    group = tiles // TILE_GROUPS
    f = lax.axis_index("face")
    t = lax.axis_index("tile")
    me = f * tiles + t
    u_me = t // group
    k_me = t % group
    right = lax.rem(t + 1, tiles)
    left = lax.rem(t + tiles - 1, tiles)
    other = 1 - f

    def at(p):
        return (p // tiles, lax.rem(p, tiles))

    def own_rows(p):
        return pl.ds(pl.multiple_of(p * per_peer, 16), per_peer)

    loads = [
        pltpu.make_async_copy(a, b, load_sem.at[i])
        for i, (a, b) in enumerate(
            (
                (winds, winds_v),
                (tracers, tracers_v),
                (metric, metric_v),
                (w_in, w_in_v),
                (aux, aux_v),
                (forcing, forcing_v),
                (w_mid, w_mid_v),
                (w_out, w_out_v),
            )
        )
    ]
    for load in loads:
        load.start()

    def signal(sem, target):
        pl.semaphore_signal(sem, inc=1, device_id=target, device_id_type=MESH)

    near_tiles = 4
    middle = min(4, tiles // near_tiles)
    high = tiles // (near_tiles * middle)
    t_low, t_middle, t_high = t % near_tiles, t // near_tiles % middle, t // (near_tiles * middle)
    along_middle = [
        t + (lax.rem(t_middle + k, middle) - t_middle) * near_tiles for k in range(1, middle)
    ]
    along_high = [
        t + (lax.rem(t_high + k, high) - t_high) * near_tiles * middle for k in range(1, high)
    ]
    along_low = [t - t_low + lax.rem(t_low + k, near_tiles) for k in range(near_tiles)]
    greeted = [(other, tile) for tile in along_low] + [(f, tile) for tile in along_low[1:]]
    greeted += [(f, tile) for tile in [right, left] + along_middle + along_high]
    barrier = pltpu.get_barrier_semaphore()
    for target in greeted:
        signal(barrier, target)

    def remote(src, dst, send, recv, target):
        copy = pltpu.make_async_remote_copy(
            src, dst, send, recv, device_id=target, device_id_type=MESH
        )
        copy.start()
        return copy

    def arrived(ref, sem):
        pltpu.make_async_copy(ref, ref, sem).wait()

    def turn_winds(h):
        for g in range(4):
            rows = [
                winds_v[pl.ds(c * 512 + h * 256 + xh * 8 + 2 * g + lo, HALF, stride=SIZE_X), :]
                for c in range(2)
                for lo in range(2)
                for xh in range(2)
            ]
            wind_b16[h, g] = jnp.concatenate(rows, axis=0).T.astype(jnp.bfloat16)

    def turn_state(h, x):
        rows = [
            tracers_v[pl.ds(i * 512 + h * 256 + xh * 8 + x, HALF, stride=SIZE_X), :]
            for xh in range(2)
            for i in range(FIELDS)
        ]
        turned = jnp.concatenate(rows, axis=0).T
        half_b16[h, x] = turned.astype(jnp.bfloat16)
        return turned

    partner = (other, t)
    loads[0].wait()
    turn_winds(other)
    loads[1].wait()
    turn_state(other, 0)
    pl.semaphore_wait(barrier, len(greeted))
    for tile in along_middle:
        signal(known.at[0], (f, tile))
    sent = [
        remote(wind_b16.at[other], wind_in.at[f], near_send.at[2], near_recv.at[2], partner)
    ]
    for x in range(8):
        if x > 0:
            turn_state(other, x)
        sent.append(
            remote(
                half_b16.at[other, x],
                state_in.at[f, x],
                near_send.at[3 + x],
                near_recv.at[3 + x],
                partner,
            )
        )
    loads[2].wait()
    face_rows = pl.ds(pl.multiple_of(f * SIZE_X, SIZE_X), SIZE_X)
    sent += [
        remote(metric_v, metric_all.at[0, face_rows], near_send.at[0], near_recv.at[0], partner),
        remote(batch_pos, pos_all.at[f], near_send.at[1], near_recv.at[1], partner),
    ]
    metric_all[0, face_rows, :] = metric_v[...]
    pos_all[f] = batch_pos[...]
    turn_winds(f)
    for x in range(8):
        state[f, x, 0:SIZE_Y, :] = turn_state(f, x)

    def send_halo(face):
        for side, tile, start in ((0, right, SIZE_Y - HALO), (1, left, 0)):
            rows = pl.ds(start, HALO)
            for kind, src, dst in (
                (0, metric_v, metric_all.at[1 + side, face_rows]),
                (1, wind_b16.at[face, :, rows], halo_wind.at[side, f]),
                (2, half_b16.at[face, :, rows], halo_state.at[side, f]),
            ):
                sent.append(
                    remote(
                        src,
                        dst,
                        halo_send.at[kind, side, face],
                        halo_recv.at[kind, side, f],
                        (face, tile),
                    )
                )

    if middle > 1:
        pl.semaphore_wait(known.at[0], middle - 1)
    for tile in along_high:
        signal(known.at[1], (f, tile))
    send_halo(f)

    def fill_place(face):
        pos = pos_all[face]
        slot = pos // COLUMNS * per_peer + pos % per_peer
        one = jnp.ones((CHUNK, SIZE_Y), jnp.bfloat16)
        zero = jnp.zeros((CHUNK, SIZE_Y), jnp.bfloat16)

        @pl.loop(0, COLUMNS // CHUNK)
        def _(i):
            rows = pl.ds(pl.multiple_of(i * CHUNK, CHUNK), CHUNK)
            index = iota((CHUNK, SIZE_Y), 0).astype(jnp.int16)
            here = slot - i * CHUNK
            for x in range(SIZE_X):
                row = jnp.broadcast_to(here[x : x + 1, :], (16, SIZE_Y)).astype(jnp.int16)
                row = jnp.concatenate([row] * (CHUNK // 16), axis=0)
                hit = jnp.where(index == row, one, zero)
                place[face, rows, x * SIZE_Y : (x + 1) * SIZE_Y] = hit

    fill_place(f)
    if high > 1:
        pl.semaphore_wait(known.at[1], high - 1)
    send_halo(other)

    loads[5].wait()
    months = day[0] * 12
    month_lo = months // 365
    month_hi = lax.rem(month_lo + 1, 12)
    part = jnp.full((1, 1, SIZE_Y), months - month_lo * 365, jnp.int32).astype(jnp.float32) / 365.0
    for c in range(0, FORC, 4):
        lower = forcing_v[pl.ds(month_lo * FORC + c, 4)].astype(jnp.float32)
        upper = forcing_v[pl.ds(month_hi * FORC + c, 4)].astype(jnp.float32)
        now = (1.0 - part) * lower + part * upper
        forc_rows[c * SIZE_X : (c + 4) * SIZE_X, :] = now.reshape(4 * SIZE_X, SIZE_Y)
    forc_rows[FORC * SIZE_X :, :] = jnp.zeros((4 * SIZE_X, SIZE_Y), jnp.float32)
    for x in range(SIZE_X):
        block = forc_rows[pl.ds(x, 48, stride=SIZE_X), :].astype(jnp.bfloat16)
        for k in (0, 64):
            forc_mat[k : k + 48, x * SIZE_Y : (x + 1) * SIZE_Y] = block
    for k in (48, 112):
        forc_mat[k : k + 16, :] = jnp.zeros((16, COLUMNS), jnp.bfloat16)

    def spread(c, out, dst, recv):
        def send(k):
            p = c * group + lax.rem(k_me + k, group)
            pltpu.make_async_remote_copy(
                out.at[own_rows(p)],
                dst.at[own_rows(me)],
                relay_send,
                recv,
                device_id=at(p),
                device_id_type=MESH,
            ).start()

        own = c == f * TILE_GROUPS + u_me

        @pl.when(own)
        def _():
            for k in range(1, group):
                send(k)
            pltpu.make_async_copy(out.at[own_rows(me)], dst.at[own_rows(me)], recv).start()

        @pl.when(jnp.logical_not(own))
        def _():
            for k in range(group):
                send(k)

    chips = devices // 2
    core = lax.rem(t, 2)
    low_lane = iota((per_peer, 128), 1) < 64

    def chip_rows(g):
        return pl.ds(pl.multiple_of(g * per_peer, 16), per_peer)

    @pl.loop(0, COLUMNS // CHUNK)
    def _(i):
        n = CHUNK // per_peer
        rows = pl.ds(pl.multiple_of(i * CHUNK, CHUNK), CHUNK)
        value = dot(place[f, rows, :], forc_mat[...], NT)
        for k in range(0, max(n, 1), 2):
            both = [value[(k + m) * per_peer : (k + m + 1) * per_peer, :] for m in range(2)]
            packed = jnp.where(low_lane, both[0], both[1]).astype(jnp.bfloat16)
            forc_out[chip_rows((i * n + k) // 2), :] = packed

    chip = me // 2

    def send_forcing(k):
        g = lax.rem(chip + k, chips)
        pltpu.make_async_remote_copy(
            forc_out.at[chip_rows(g)],
            forc_in.at[core, chip_rows(chip)],
            forc_send.at[0],
            forc_recv.at[0],
            device_id=at(2 * g + core),
            device_id_type=MESH,
        ).start()

    def spread_bias(ref, into, size):
        for k in range(0, size, 128):
            n = min(128, size - k)
            into[k : k + n, :] = jnp.broadcast_to(ref[k : k + n].reshape(1, n), (128, n)).T

    spread_bias(b_in, bias_in, HIDDEN)
    spread_bias(b_mid, bias_mid, HIDDEN)
    spread_bias(b_out, bias_out, OUT)
    loads[3].wait()
    w_aux[...] = w_in_v[CHANNELS + FORC :, :].T
    row = iota((CHANNELS, 128), 0)
    pick = (iota((CHANNELS, 128), 1) == row + core * 64) & (row < FORC)
    w_forc[...] = dot(
        w_in_v[CHANNELS : 2 * CHANNELS, :], pick.astype(jnp.bfloat16), TN
    ).astype(jnp.bfloat16)
    lane = iota((CHANNELS, 512), 1)
    ch = (lane // 16) % 4 * LEVELS + lane // 128 % 2 * HALF + lane % 16
    pick = (iota((CHANNELS, 512), 0) == ch) & (lane // 64 % 2 == lane // 256)
    w_dyn[...] = dot(w_in_v[0:CHANNELS, :], pick.astype(jnp.bfloat16), TN).astype(jnp.bfloat16)
    loads[4].wait()

    def twice(one, two=None):
        return jnp.concatenate([one, one if two is None else two], axis=1)

    @pl.loop(0, COLUMNS // CHUNK)
    def _(i):
        cols = pl.ds(pl.multiple_of(i * CHUNK, CHUNK), CHUNK)
        pre[:, cols] = dot(w_aux[...], aux_v[:, cols]) + twice(bias_in[...])

    arrived(pos_all.at[0], near_recv.at[1])
    fill_place(other)

    arrived(metric_all.at[0, pl.ds(0, SIZE_X)], near_recv.at[0])
    for face in range(2):
        for side in range(2):
            arrived(metric_all.at[1 + side, pl.ds(0, SIZE_X)], halo_recv.at[0, side, face])

    def node_weight(shape, dim):
        n = iota(shape, dim) % 4
        return jnp.where((n == 0) | (n == 3), np.float32(1.0 / 6.0), np.float32(5.0 / 6.0))

    turned = []
    for k in range(3):
        block = metric_all[k] * node_weight((32, SIZE_Y), 0) * node_weight((32, SIZE_Y), 1)
        turned.append(jnp.concatenate([block] * 4, axis=0).T)
    points = jnp.concatenate([turned[0], turned[2][:HALO], turned[1][SIZE_Y - HALO :]], axis=0)
    node_x = iota((WIDE, 128), 1) % 4
    node_y = iota((WIDE, 128), 0) % 4
    along = points + jnp.where(node_x == 0, pltpu.roll(points, 1, 1), 0.0)
    along = along + jnp.where(node_x == 3, pltpu.roll(points, 127, 1), 0.0)
    both = along + jnp.where(node_y == 0, pltpu.roll(along, 1, 0), 0.0)
    both = both + jnp.where(node_y == 3, pltpu.roll(along, WIDE - 1, 0), 0.0)
    scaled, inverted = -time_step * points, 1.0 / both
    low = iota((WIDE, 128), 1) < 64
    for face in range(2):
        for x in range(8):
            k = face * SIZE_X + x
            for value, into in ((scaled, mass), (inverted, inverse)):
                one = jnp.broadcast_to(value[:, k : k + 1], (WIDE, 128))
                two = jnp.broadcast_to(value[:, k + 8 : k + 9], (WIDE, 128))
                into[face, x] = jnp.where(low, one, two)

    wind_in[f] = wind_b16[f]
    out_lane = iota((128, 512), 1)
    from_lane = out_lane // 128 * 32 + out_lane // 64 % 2 * 16 + out_lane % 16
    widen = (iota((128, 512), 0) == from_lane).astype(jnp.bfloat16)
    for kind in (1, 2):
        for face in range(2):
            for side in range(2):
                ref = (halo_wind, halo_state)[kind - 1].at[side, face]
                arrived(ref, halo_recv.at[kind, side, face])
    arrived(wind_in.at[0], near_recv.at[2])
    for face in range(2):
        for g in range(4):
            rows = jnp.concatenate(
                [wind_in[face, g], halo_wind[1, face, g], halo_wind[0, face, g]], axis=0
            )
            wide = dot(rows, widen)
            for c in range(2):
                for lo in range(2):
                    k = 2 * c + lo
                    x = 2 * g + lo
                    wind[c, face, x] = wide[:, k * 128 : (k + 1) * 128] * mass[face, x]
    for face in range(2):
        state[face, :, SIZE_Y : SIZE_Y + HALO, :] = halo_state[1, face].astype(jnp.float32)
        state[face, :, SIZE_Y + HALO :, :] = halo_state[0, face].astype(jnp.float32)
    for x in range(8):
        arrived(state_in.at[0, x], near_recv.at[3 + x])
        state[other, x, 0:SIZE_Y, :] = state_in[other, x].astype(jnp.float32)

    low_half = iota((NODES, 128), 1) < 64

    @pl.loop(0, SUBSTEPS)
    def _(step):
        few = chips // 2

        @pl.when(step < 2)
        def _():
            for k in range(1, few):
                send_forcing(step * few + k)

        @pl.when(step == 1)
        def _():
            send_forcing(few)

        @pl.when(step == 0)
        def _():
            pltpu.make_async_copy(
                forc_out.at[chip_rows(chip)], forc_in.at[core, chip_rows(chip)], forc_recv.at[0]
            ).start()

        @pl.loop(0, NODES // 8)
        def _(i):
            for face in range(2):
                for e in range(0, 8, 4):

                    def rows(j):
                        return pl.ds(i * 32 + j, 8, stride=4)

                    s = [[state[face, e + a, rows(j), :] for j in range(4)] for a in range(4)]
                    along_y = [derivative(s[a]) for a in range(4)]
                    for j in range(4):
                        along_x = derivative([s[a][j] for a in range(4)])
                        for a in range(4):
                            value = wind[0, face, e + a, rows(j), :] * along_x[a]
                            value = value + wind[1, face, e + a, rows(j), :] * along_y[a][j]
                            rate[face, e + a, j, pl.ds(pl.multiple_of(i * 8, 8), 8), :] = value

        def summed(face, x, j):
            value = rate[face, x, j]
            if x == 3:
                return value + rate[face, 4, j]
            if x == 4:
                return rate[face, 3, j] + value
            if x == 7:
                pair = jnp.where(low_half, rate[1 - face, 0, j], rate[face, 0, j])
                return value + pltpu.roll(pair, 64, 1)
            if x == 0:
                pair = jnp.where(low_half, rate[face, 7, j], rate[1 - face, 7, j])
                return value + pltpu.roll(pair, 64, 1)
            return value

        for face in range(2):
            for x in range(8):
                z = [summed(face, x, j) for j in range(4)]
                z[0], z[3] = (
                    z[0] + pltpu.roll(z[3], 1, 0),
                    z[3] + pltpu.roll(z[0], NODES - 1, 0),
                )
                for j in range(4):
                    rows = pl.ds(j, NODES, stride=4)
                    state[face, x, rows, :] = (
                        state[face, x, rows, :] + z[j] * inverse[face, x, rows, :]
                    )

    for face in range(2):
        for x in range(8):
            dyn[face, x * SIZE_Y : (x + 1) * SIZE_Y, :] = state[face, x, 0:SIZE_Y, :].astype(
                jnp.bfloat16
            )

    low_row = iota((2 * CHUNK, 128), 1) < 64

    @pl.loop(0, TILE_GROUPS)
    def _(i):
        u = lax.rem(u_me + stage(i), TILE_GROUPS)
        chunks = [(other * TILE_GROUPS + u), (f * TILE_GROUPS + u)]
        rows = [pl.ds(pl.multiple_of(c * CHUNK, CHUNK), CHUNK) for c in chunks]
        q = [
            [
                dot(
                    jnp.concatenate(
                        [place[face, r, xh * 1024 : (xh + 1) * 1024] for r in rows], axis=0
                    ),
                    dyn[face],
                )
                for xh in range(2)
            ]
            for face in range(2)
        ]
        turn = pltpu.roll(jnp.where(low_row, q[1][0], q[0][1]), 64, 1)
        packed = (jnp.where(low_row, q[0][0], q[1][1]) + turn).astype(jnp.bfloat16)
        for k in range(2):
            dyn_out[rows[k], :] = packed[k * CHUNK : (k + 1) * CHUNK, :]
            spread(chunks[k], dyn_out, dyn_in, dyn_recv.at[f * TILE_GROUPS + u_me])

    arrived(forc_in.at[core], forc_recv.at[0])
    sent.append(
        remote(
            forc_in.at[core],
            forc_in.at[core],
            forc_send.at[1],
            forc_recv.at[1],
            at(2 * chip + 1 - core),
        )
    )
    arrived(forc_in.at[1 - core], forc_recv.at[1])

    @pl.loop(0, COLUMNS // CHUNK)
    def _(i):
        cols = pl.ds(pl.multiple_of(i * CHUNK, CHUNK), CHUNK)
        half = CHUNK // 2
        blocks = []
        for k in range(0, half, per_peer):
            rows = pl.ds(pl.multiple_of(i * half + k, 16), per_peer)
            blocks += [forc_in[0, rows, :], forc_in[1, rows, :]]
        pre[:, cols] += dot(w_forc[...], jnp.concatenate(blocks, axis=0), NT)

    loads[6].wait()
    loads[7].wait()
    level_lane = iota((256, CHANNELS), 1)
    level_row = iota((256, CHANNELS), 0)

    @pl.loop(0, TILE_GROUPS)
    def _(i):
        u = lax.rem(u_me + stage(i), TILE_GROUPS)
        chunks = [
            pl.ds(pl.multiple_of((h * TILE_GROUPS + u) * CHUNK, CHUNK), CHUNK) for h in range(2)
        ]
        for h in range(2):
            arrived(dyn_in.at[chunks[h]], dyn_recv.at[h * TILE_GROUPS + u])
        block = jnp.concatenate([dyn_in[chunks[0], :], dyn_in[chunks[1], :]], axis=1)
        turned = block.T
        hidden = [
            leaky(pre[:, chunks[face]] + dot(w_dyn[:, face * 256 : (face + 1) * 256], turned))
            for face in range(2)
        ]
        hidden = twice(*hidden).astype(jnp.bfloat16)
        hidden = leaky(dot(w_mid_v[...], hidden) + twice(twice(bias_mid[...])))
        result = dot(w_out_v[...], hidden.astype(jnp.bfloat16)) + twice(twice(bias_out[...]))
        result = result.astype(jnp.bfloat16)
        for face in range(2):
            part = result[:, face * CHUNK : (face + 1) * CHUNK]
            diag_v[:, chunks[face]] = part[CHANNELS:, :]
            row = level_lane // LEVELS * 16 + level_lane % 16
            row = row + level_lane // HALF % 2 * 128 + face * 64
            pick = (level_row == row).astype(jnp.bfloat16)
            change = part[0:CHANNELS, :].astype(jnp.float32).T
            value = dot(block, pick) + physics_weight * change
            back_out[chunks[face], :] = value.astype(jnp.bfloat16)
        for face in (other, f):
            c = face * TILE_GROUPS + u
            spread(c, back_out, back_in, back_recv.at[f * TILE_GROUPS + u_me])

    diag_copy = pltpu.make_async_copy(diag_v, diagnostics, out_sem.at[0])
    diag_copy.start()

    for v in (2, 1, 3, 0):
        u = lax.rem(u_me + TILE_GROUPS - v, TILE_GROUPS)
        parts = []
        for face in range(2):
            c = face * TILE_GROUPS + u
            rows = pl.ds(pl.multiple_of(c * CHUNK, CHUNK), CHUNK)
            arrived(back_in.at[rows], back_recv.at[c])
            parts.append((back_in[rows, :], rows))
        for k in range(0, COLUMNS, 512):
            value = sum(dot(back, place[f, rows, k : k + 512], TN) for back, rows in parts)
            value = value.astype(jnp.bfloat16)
            total[:, k : k + 512] = value if v == 2 else total[:, k : k + 512] + value
    updated_copy = pltpu.make_async_copy(total, updated, out_sem.at[1])
    updated_copy.start()
    for copy in sent:
        copy.wait_send()
    away = pl.ds(0, (devices - 1) * per_peer)
    for out in (dyn_out, back_out):
        arrived(out.at[away], relay_send)
    arrived(forc_out.at[pl.ds(0, (chips - 1) * per_peer)], forc_send.at[0])
    diag_copy.wait()
    updated_copy.wait()


PIECES = 4


def finish(new, diag, updated, diagnostics, new_v, diag_v, updated_v, load_sem, out_sem):
    n, d = CHANNELS // PIECES, (OUT - CHANNELS) // PIECES // 16 * 16
    cuts = [pl.ds(k * n, n) for k in range(PIECES)]
    cuts += [pl.ds(k * d, d if k < PIECES - 1 else OUT - CHANNELS - k * d) for k in range(PIECES)]
    ends = ((new, new_v),) * PIECES + ((diag, diag_v),) * PIECES
    loads = [
        pltpu.make_async_copy(src.at[cut], dst.at[cut], load_sem.at[k])
        for k, (cut, (src, dst)) in enumerate(zip(cuts, ends))
    ]
    for copy in loads:
        copy.start()
    outs = []

    def out(src, dst):
        outs.append(pltpu.make_async_copy(src, dst, out_sem.at[len(outs)]))
        outs[-1].start()

    for k in range(PIECES):
        loads[k].wait()
        for x in range(SIZE_X):
            block = new_v[k * n : (k + 1) * n, x * SIZE_Y : (x + 1) * SIZE_Y]
            updated_v[pl.ds(k * n * SIZE_X + x, n, stride=SIZE_X), :] = block.astype(jnp.float32)
        rows = pl.ds(k * n * SIZE_X, n * SIZE_X)
        out(updated_v.at[rows], updated.at[rows])
    for k in range(PIECES, 2 * PIECES):
        loads[k].wait()
        out(diag_v.at[cuts[k]], diagnostics.at[cuts[k]])
    for copy in outs:
        copy.wait()


def local(
    tracers,
    wind_field,
    metric,
    forcing,
    aux_inputs,
    batch_pos,
    day_of_year,
    w_in,
    b_in,
    w_mid,
    b_mid,
    w_out,
    b_out,
):
    tiles = lax.axis_size("tile")
    anywhere = pl.BlockSpec(memory_space=pl.ANY)
    vmem = pl.BlockSpec(memory_space=pltpu.VMEM)
    f32, b16 = jnp.float32, jnp.bfloat16
    dma = pltpu.SemaphoreType.DMA
    scratch = [
        pltpu.VMEM((CHANNELS * SIZE_X, SIZE_Y), f32),
        pltpu.VMEM((2 * LEVELS * SIZE_X, SIZE_Y), f32),
        pltpu.VMEM((SIZE_X, SIZE_Y), f32),
        pltpu.VMEM((12 * FORC, SIZE_X, SIZE_Y), b16),
        pltpu.VMEM((AUX, COLUMNS), b16),
        pltpu.VMEM(w_in.shape[::-1], b16),
        pltpu.VMEM(w_mid.shape, b16),
        pltpu.VMEM(w_out.shape, b16),
        dma((8,)),
        pltpu.VMEM((2, 8, SIZE_Y, 128), b16),
        pltpu.VMEM((2, 4, SIZE_Y, 128), b16),
        pltpu.VMEM((2, 8, SIZE_Y, 128), b16),
        pltpu.VMEM((2, 4, SIZE_Y, 128), b16),
        pltpu.VMEM((2, 2, 8, HALO, 128), b16),
        pltpu.VMEM((2, 2, 4, HALO, 128), b16),
        pltpu.VMEM((3, 2 * SIZE_X, SIZE_Y), f32),
        pltpu.VMEM((2, SIZE_X, SIZE_Y), jnp.int32),
        pltpu.VMEM((2, 8, WIDE, 128), f32),
        pltpu.VMEM((2, 2, 8, WIDE, 128), f32),
        pltpu.VMEM((2, 8, WIDE, 128), f32),
        pltpu.VMEM((2, 8, WIDE, 128), f32),
        pltpu.VMEM((2, 8, 4, NODES, 128), f32),
        pltpu.VMEM((2, COLUMNS, COLUMNS), b16),
        pltpu.VMEM((48 * SIZE_X, SIZE_Y), f32),
        pltpu.VMEM((128, COLUMNS), b16),
        pltpu.VMEM((COLUMNS // 2, 128), b16),
        pltpu.VMEM((2, COLUMNS // 2, 128), b16),
        pltpu.VMEM((2, COLUMNS // 2, 128), b16),
        pltpu.VMEM((COLUMNS, 128), b16),
        pltpu.VMEM((COLUMNS, 128), b16),
        pltpu.VMEM((COLUMNS, 128), b16),
        pltpu.VMEM((COLUMNS, 128), b16),
        pltpu.VMEM((HIDDEN, COLUMNS), f32),
        pltpu.VMEM((HIDDEN, AUX), b16),
        pltpu.VMEM((HIDDEN, 128), b16),
        pltpu.VMEM((HIDDEN, 512), b16),
        pltpu.VMEM((HIDDEN, 128), f32),
        pltpu.VMEM((HIDDEN, 128), f32),
        pltpu.VMEM((OUT, 128), f32),
        pltpu.VMEM((OUT - CHANNELS, COLUMNS), b16),
        pltpu.VMEM((CHANNELS, COLUMNS), b16),
        pltpu.SemaphoreType.REGULAR((2,)),
        dma((11,)),
        dma((11,)),
        dma((3, 2, 2)),
        dma((3, 2, 2)),
        dma,
        dma((2,)),
        dma((2,)),
        dma((2 * TILE_GROUPS,)),
        dma((2 * TILE_GROUPS,)),
        dma((2,)),
    ]
    updated, diagnostics = pl.pallas_call(
        functools.partial(kernel, tiles),
        out_shape=(
            jax.ShapeDtypeStruct((CHANNELS, COLUMNS), b16),
            jax.ShapeDtypeStruct((OUT - CHANNELS, COLUMNS), b16),
        ),
        in_specs=[
            anywhere,
            anywhere,
            anywhere,
            anywhere,
            anywhere,
            vmem,
            pl.BlockSpec(memory_space=pltpu.SMEM),
            anywhere,
            vmem,
            anywhere,
            vmem,
            anywhere,
            vmem,
        ],
        out_specs=(anywhere, anywhere),
        scratch_shapes=scratch,
        compiler_params=pltpu.CompilerParams(
            collective_id=0, has_side_effects=True, vmem_limit_bytes=60 * 2**20
        ),
    )(
        tracers.reshape(CHANNELS * SIZE_X, SIZE_Y),
        wind_field.reshape(2 * LEVELS * SIZE_X, SIZE_Y),
        metric,
        forcing.reshape(12 * FORC, SIZE_X, SIZE_Y),
        aux_inputs,
        batch_pos,
        day_of_year,
        w_in.T,
        b_in,
        w_mid,
        b_mid,
        w_out,
        b_out,
    )
    updated, diagnostics = pl.pallas_call(
        finish,
        out_shape=(
            jax.ShapeDtypeStruct((CHANNELS * SIZE_X, SIZE_Y), f32),
            jax.ShapeDtypeStruct((OUT - CHANNELS, COLUMNS), b16),
        ),
        in_specs=[anywhere, anywhere],
        out_specs=(anywhere, anywhere),
        scratch_shapes=[
            pltpu.VMEM((CHANNELS, COLUMNS), b16),
            pltpu.VMEM((OUT - CHANNELS, COLUMNS), b16),
            pltpu.VMEM((CHANNELS * SIZE_X, SIZE_Y), f32),
            dma((2 * PIECES,)),
            dma((2 * PIECES,)),
        ],
        compiler_params=pltpu.CompilerParams(vmem_limit_bytes=60 * 2**20),
    )(updated, diagnostics)
    return updated.reshape(tracers.shape), diagnostics


def solution(mesh):
    placed = (
        P(None, None, "face", "tile"),
        P(None, None, "face", "tile"),
        P("face", "tile"),
        P(None, None, "face", "tile"),
        P(None, ("face", "tile")),
        P("face", "tile"),
        P(),
        P(),
        P(),
        P(),
        P(),
        P(),
        P(),
    )
    return jax.shard_map(
        local,
        mesh=mesh,
        in_specs=placed,
        out_specs=(P(None, None, "face", "tile"), P(None, ("face", "tile"))),
        check_vma=False,
    )
```

```python
import functools

import jax
import jax.numpy as jnp
import numpy as np
from jax import lax
from jax.experimental import pallas as pl
from jax.experimental.pallas import tpu as pltpu
from jax.sharding import PartitionSpec as P

SUBSTEPS = 4
FIELDS = 4
LEVELS = 32
HALF = 16
SIZE_X = 16
SIZE_Y = 128
COLUMNS = SIZE_X * SIZE_Y
CHANNELS = FIELDS * LEVELS
FORC = 44
AUX = 384
HIDDEN = 512
OUT = 368
HALO = 16
WIDE = SIZE_Y + 2 * HALO
NODES = WIDE // 4
CHUNK = 256
TILE_GROUPS = 4

MESH = pl.DeviceIdType.MESH
leak_slope = 0.15
time_step = 0.05
physics_weight = 0.5

root = np.sqrt(5.0)
big = 5.0 * (root + 1.0) / 4.0
mid = 5.0 * (root - 1.0) / 4.0
near = (root + 1.0) / 4.0
far = (root - 1.0) / 4.0


def derivative(s):
    c, d = s[0] - s[3], s[1] - s[2]
    e = (s[1] + s[2]) - (s[0] + s[3])
    p = (-1.75) * c + ((big + mid) / 2.0) * d
    q = (-(near - far) / 2.0) * c - (root / 4.0) * d
    outer, inner = 1.25 * e, (root / 4.0) * e
    return [p + outer, q + inner, q - inner, p - outer]


def leaky(value):
    return jnp.where(value > 0, value, leak_slope * value)


def iota(shape, dim):
    return lax.broadcasted_iota(jnp.int32, shape, dim)


def dot(a, b, contract=((1,), (0,))):
    return lax.dot_general(a, b, (contract, ((), ())), preferred_element_type=jnp.float32)


def stage(i):
    a = (i + 1) // 2
    pair = a % 2
    return (2 - a, 1 - pair * (i - 1)), (2 - a + 2 * pair, pair * (2 - i))


NT = ((1,), (1,))
TN = ((0,), (0,))


def kernel(
    tiles,
    tracers,
    winds,
    metric,
    forcing,
    aux,
    batch_pos,
    day,
    w_in,
    b_in,
    w_mid,
    b_mid,
    w_out,
    b_out,
    updated,
    diagnostics,
    tracers_v,
    winds_v,
    metric_v,
    forcing_v,
    aux_v,
    w_in_v,
    w_mid_v,
    w_out_v,
    pos_v,
    day_v,
    b_in_v,
    b_mid_v,
    b_out_v,
    load_sem,
    half_b16,
    wind_b16,
    state_in,
    wind_in,
    halo_state,
    halo_wind,
    metric_all,
    pos_all,
    state,
    wind,
    mass,
    inverse,
    rate,
    place,
    forc_rows,
    forc_mat,
    forc_out,
    forc_in,
    dyn,
    dyn_out,
    dyn_in,
    back_out,
    back_in,
    pre,
    w_aux,
    w_forc,
    w_dyn,
    bias_in,
    bias_mid,
    bias_out,
    diag_v,
    total,
    known,
    near_send,
    near_recv,
    halo_send,
    halo_recv,
    relay_send,
    forc_send,
    forc_recv,
    dyn_recv,
    back_recv,
    out_sem,
):
    devices = 2 * tiles
    per_peer = COLUMNS // devices
    group = tiles // TILE_GROUPS
    f = lax.axis_index("face")
    t = lax.axis_index("tile")
    me = f * tiles + t
    u_me = t // group
    k_me = t % group
    right = lax.rem(t + 1, tiles)
    left = lax.rem(t + tiles - 1, tiles)
    other = 1 - f

    def at(p):
        return (p // tiles, lax.rem(p, tiles))

    def own_rows(p):
        return pl.ds(pl.multiple_of(p * per_peer, 16), per_peer)

    loads = [
        pltpu.make_async_copy(a, b, load_sem.at[i])
        for i, (a, b) in enumerate(
            (
                (winds, winds_v),
                (tracers, tracers_v),
                (metric, metric_v),
                (w_in, w_in_v),
                (aux, aux_v),
                (forcing, forcing_v),
                (w_mid, w_mid_v),
                (w_out, w_out_v),
                (batch_pos, pos_v),
                (day, day_v),
                (b_in, b_in_v),
                (b_mid, b_mid_v),
                (b_out, b_out_v),
            )
        )
    ]
    for load in loads:
        load.start()

    def signal(sem, target):
        pl.semaphore_signal(sem, inc=1, device_id=target, device_id_type=MESH)

    near_tiles = 4
    middle = min(4, tiles // near_tiles)
    high = tiles // (near_tiles * middle)
    t_low, t_middle, t_high = t % near_tiles, t // near_tiles % middle, t // (near_tiles * middle)
    along_middle = [
        t + (lax.rem(t_middle + k, middle) - t_middle) * near_tiles for k in range(1, middle)
    ]
    along_high = [
        t + (lax.rem(t_high + k, high) - t_high) * near_tiles * middle for k in range(1, high)
    ]
    along_low = [t - t_low + lax.rem(t_low + k, near_tiles) for k in range(near_tiles)]
    greeted = [(other, tile) for tile in along_low] + [(f, tile) for tile in along_low[1:]]
    greeted += [(f, tile) for tile in [right, left] + along_middle + along_high]
    barrier = pltpu.get_barrier_semaphore()
    for target in greeted:
        signal(barrier, target)

    def remote(src, dst, send, recv, target):
        copy = pltpu.make_async_remote_copy(
            src, dst, send, recv, device_id=target, device_id_type=MESH
        )
        copy.start()
        return copy

    def arrived(ref, sem):
        pltpu.make_async_copy(ref, ref, sem).wait()

    def turn_winds(h):
        for g in range(4):
            rows = [
                winds_v[pl.ds(c * 512 + h * 256 + xh * 8 + 2 * g + lo, HALF, stride=SIZE_X), :]
                for c in range(2)
                for lo in range(2)
                for xh in range(2)
            ]
            wind_b16[h, g] = jnp.concatenate(rows, axis=0).T.astype(jnp.bfloat16)

    def turn_state(h, x):
        rows = [
            tracers_v[pl.ds(i * 512 + h * 256 + xh * 8 + x, HALF, stride=SIZE_X), :]
            for xh in range(2)
            for i in range(FIELDS)
        ]
        turned = jnp.concatenate(rows, axis=0).T
        half_b16[h, x] = turned.astype(jnp.bfloat16)
        return turned

    partner = (other, t)
    loads[0].wait()
    turn_winds(other)
    loads[1].wait()
    turn_state(other, 0)
    pl.semaphore_wait(barrier, len(greeted))
    for tile in along_middle:
        signal(known.at[0], (f, tile))
    sent = [
        remote(wind_b16.at[other], wind_in.at[f], near_send.at[2], near_recv.at[2], partner)
    ]
    for x in range(8):
        if x > 0:
            turn_state(other, x)
        sent.append(
            remote(
                half_b16.at[other, x],
                state_in.at[f, x],
                near_send.at[3 + x],
                near_recv.at[3 + x],
                partner,
            )
        )
    loads[2].wait()
    loads[8].wait()
    face_rows = pl.ds(pl.multiple_of(f * SIZE_X, SIZE_X), SIZE_X)
    sent += [
        remote(metric_v, metric_all.at[0, face_rows], near_send.at[0], near_recv.at[0], partner),
        remote(pos_v, pos_all.at[f], near_send.at[1], near_recv.at[1], partner),
    ]
    metric_all[0, face_rows, :] = metric_v[...]
    pos_all[f] = pos_v[...]
    turn_winds(f)
    for x in range(8):
        state[f, x, 0:SIZE_Y, :] = turn_state(f, x)

    def send_halo(face):
        for side, tile, start in ((0, right, SIZE_Y - HALO), (1, left, 0)):
            rows = pl.ds(start, HALO)
            for kind, src, dst in (
                (0, metric_v, metric_all.at[1 + side, face_rows]),
                (1, wind_b16.at[face, :, rows], halo_wind.at[side, f]),
                (2, half_b16.at[face, :, rows], halo_state.at[side, f]),
            ):
                sent.append(
                    remote(
                        src,
                        dst,
                        halo_send.at[kind, side, face],
                        halo_recv.at[kind, side, f],
                        (face, tile),
                    )
                )

    if middle > 1:
        pl.semaphore_wait(known.at[0], middle - 1)
    for tile in along_high:
        signal(known.at[1], (f, tile))
    send_halo(f)

    def fill_place(face):
        pos = pos_all[face]
        slot = pos // COLUMNS * per_peer + pos % per_peer
        one = jnp.ones((CHUNK, SIZE_Y), jnp.bfloat16)
        zero = jnp.zeros((CHUNK, SIZE_Y), jnp.bfloat16)

        @pl.loop(0, COLUMNS // CHUNK)
        def _(i):
            rows = pl.ds(pl.multiple_of(i * CHUNK, CHUNK), CHUNK)
            index = iota((CHUNK, SIZE_Y), 0).astype(jnp.int16)
            here = slot - i * CHUNK
            for x in range(SIZE_X):
                row = jnp.broadcast_to(here[x : x + 1, :], (16, SIZE_Y)).astype(jnp.int16)
                row = jnp.concatenate([row] * (CHUNK // 16), axis=0)
                hit = jnp.where(index == row, one, zero)
                place[face, rows, x * SIZE_Y : (x + 1) * SIZE_Y] = hit

    fill_place(f)
    if high > 1:
        pl.semaphore_wait(known.at[1], high - 1)
    send_halo(other)

    loads[5].wait()
    loads[9].wait()
    months = day_v[0] * 12
    month_lo = months // 365
    month_hi = lax.rem(month_lo + 1, 12)
    part = jnp.full((1, 1, SIZE_Y), months - month_lo * 365, jnp.int32).astype(jnp.float32) / 365.0
    for c in range(0, FORC, 4):
        lower = forcing_v[pl.ds(month_lo * FORC + c, 4)].astype(jnp.float32)
        upper = forcing_v[pl.ds(month_hi * FORC + c, 4)].astype(jnp.float32)
        now = (1.0 - part) * lower + part * upper
        forc_rows[c * SIZE_X : (c + 4) * SIZE_X, :] = now.reshape(4 * SIZE_X, SIZE_Y)
    forc_rows[FORC * SIZE_X :, :] = jnp.zeros((4 * SIZE_X, SIZE_Y), jnp.float32)
    for x in range(SIZE_X):
        block = forc_rows[pl.ds(x, 48, stride=SIZE_X), :].astype(jnp.bfloat16)
        for k in (0, 64):
            forc_mat[k : k + 48, x * SIZE_Y : (x + 1) * SIZE_Y] = block
    for k in (48, 112):
        forc_mat[k : k + 16, :] = jnp.zeros((16, COLUMNS), jnp.bfloat16)

    low_size = min(near_tiles, group)
    z_size = group // low_size
    z_me = k_me // low_size
    far_first = sorted(range(group), key=lambda k: -min(k // low_size, z_size - k // low_size))

    def spread(i, pair, out, dst, recv):
        def send(c, k):
            p = c * group + (z_me + k // low_size) % z_size * low_size + (k_me + k) % low_size
            pltpu.make_async_remote_copy(
                out.at[own_rows(p)],
                dst.at[own_rows(me)],
                relay_send,
                recv,
                device_id=at(p),
                device_id_type=MESH,
            ).start()

        @pl.when(i == TILE_GROUPS - 1)
        def _():
            for k in far_first:
                send(pair[0], k)
                if k > 0:
                    send(pair[1], k)
            pltpu.make_async_copy(out.at[own_rows(me)], dst.at[own_rows(me)], recv).start()

        @pl.when(i < TILE_GROUPS - 1)
        def _():
            for k in far_first:
                for c in pair:
                    send(c, k)

    def chunks_of(i):
        found = []
        for on, away in stage(i):
            face, u = lax.rem(f + away, 2), lax.rem(u_me + on, TILE_GROUPS)
            found.append((face * TILE_GROUPS + u, face, u))
        return found

    def chunk_rows(c):
        return pl.ds(pl.multiple_of(c * CHUNK, CHUNK), CHUNK)

    chips = devices // 2
    core = lax.rem(t, 2)
    low_lane = iota((per_peer, 128), 1) < 64

    def chip_rows(g):
        return pl.ds(pl.multiple_of(g * per_peer, 16), per_peer)

    @pl.loop(0, COLUMNS // CHUNK)
    def _(i):
        n = CHUNK // per_peer
        rows = pl.ds(pl.multiple_of(i * CHUNK, CHUNK), CHUNK)
        value = dot(place[f, rows, :], forc_mat[...], NT)
        for k in range(0, max(n, 1), 2):
            both = [value[(k + m) * per_peer : (k + m + 1) * per_peer, :] for m in range(2)]
            packed = jnp.where(low_lane, both[0], both[1]).astype(jnp.bfloat16)
            forc_out[chip_rows((i * n + k) // 2), :] = packed

    chip = me // 2

    def send_forcing(k):
        g = lax.rem(chip + k, chips)
        pltpu.make_async_remote_copy(
            forc_out.at[chip_rows(g)],
            forc_in.at[core, chip_rows(chip)],
            forc_send.at[0],
            forc_recv.at[0],
            device_id=at(2 * g + core),
            device_id_type=MESH,
        ).start()

    def spread_bias(ref, into, size):
        for k in range(0, size, 128):
            n = min(128, size - k)
            into[k : k + n, :] = jnp.broadcast_to(ref[k : k + n].reshape(1, n), (128, n)).T

    for load in loads[10:]:
        load.wait()
    spread_bias(b_in_v, bias_in, HIDDEN)
    spread_bias(b_mid_v, bias_mid, HIDDEN)
    spread_bias(b_out_v, bias_out, OUT)
    loads[3].wait()
    w_aux[...] = w_in_v[CHANNELS + FORC :, :].T
    row = iota((CHANNELS, 128), 0)
    pick = (iota((CHANNELS, 128), 1) == row + core * 64) & (row < FORC)
    w_forc[...] = dot(
        w_in_v[CHANNELS : 2 * CHANNELS, :], pick.astype(jnp.bfloat16), TN
    ).astype(jnp.bfloat16)
    lane = iota((CHANNELS, 512), 1)
    ch = (lane // 16) % 4 * LEVELS + lane // 128 % 2 * HALF + lane % 16
    pick = (iota((CHANNELS, 512), 0) == ch) & (lane // 64 % 2 == lane // 256)
    w_dyn[...] = dot(w_in_v[0:CHANNELS, :], pick.astype(jnp.bfloat16), TN).astype(jnp.bfloat16)
    loads[4].wait()

    def twice(one, two=None):
        return jnp.concatenate([one, one if two is None else two], axis=1)

    @pl.loop(0, COLUMNS // CHUNK)
    def _(i):
        cols = pl.ds(pl.multiple_of(i * CHUNK, CHUNK), CHUNK)
        pre[:, cols] = dot(w_aux[...], aux_v[:, cols]) + twice(bias_in[...])

    arrived(pos_all.at[0], near_recv.at[1])
    fill_place(other)

    arrived(metric_all.at[0, pl.ds(0, SIZE_X)], near_recv.at[0])
    for face in range(2):
        for side in range(2):
            arrived(metric_all.at[1 + side, pl.ds(0, SIZE_X)], halo_recv.at[0, side, face])

    def node_weight(shape, dim):
        n = iota(shape, dim) % 4
        return jnp.where((n == 0) | (n == 3), np.float32(1.0 / 6.0), np.float32(5.0 / 6.0))

    turned = []
    for k in range(3):
        block = metric_all[k] * node_weight((32, SIZE_Y), 0) * node_weight((32, SIZE_Y), 1)
        turned.append(jnp.concatenate([block] * 4, axis=0).T)
    points = jnp.concatenate([turned[0], turned[2][:HALO], turned[1][SIZE_Y - HALO :]], axis=0)
    node_x = iota((WIDE, 128), 1) % 4
    node_y = iota((WIDE, 128), 0) % 4
    along = points + jnp.where(node_x == 0, pltpu.roll(points, 1, 1), 0.0)
    along = along + jnp.where(node_x == 3, pltpu.roll(points, 127, 1), 0.0)
    both = along + jnp.where(node_y == 0, pltpu.roll(along, 1, 0), 0.0)
    both = both + jnp.where(node_y == 3, pltpu.roll(along, WIDE - 1, 0), 0.0)
    scaled, inverted = -time_step * points, 1.0 / both
    low = iota((WIDE, 128), 1) < 64
    for face in range(2):
        for x in range(8):
            k = face * SIZE_X + x
            for value, into in ((scaled, mass), (inverted, inverse)):
                one = jnp.broadcast_to(value[:, k : k + 1], (WIDE, 128))
                two = jnp.broadcast_to(value[:, k + 8 : k + 9], (WIDE, 128))
                into[face, x] = jnp.where(low, one, two)

    wind_in[f] = wind_b16[f]
    out_lane = iota((128, 512), 1)
    from_lane = out_lane // 128 * 32 + out_lane // 64 % 2 * 16 + out_lane % 16
    widen = (iota((128, 512), 0) == from_lane).astype(jnp.bfloat16)
    for kind in (1, 2):
        for face in range(2):
            for side in range(2):
                ref = (halo_wind, halo_state)[kind - 1].at[side, face]
                arrived(ref, halo_recv.at[kind, side, face])
    arrived(wind_in.at[0], near_recv.at[2])
    for face in range(2):
        for g in range(4):
            rows = jnp.concatenate(
                [wind_in[face, g], halo_wind[1, face, g], halo_wind[0, face, g]], axis=0
            )
            wide = dot(rows, widen)
            for c in range(2):
                for lo in range(2):
                    k = 2 * c + lo
                    x = 2 * g + lo
                    wind[c, face, x] = wide[:, k * 128 : (k + 1) * 128] * mass[face, x]
    for face in range(2):
        state[face, :, SIZE_Y : SIZE_Y + HALO, :] = halo_state[1, face].astype(jnp.float32)
        state[face, :, SIZE_Y + HALO :, :] = halo_state[0, face].astype(jnp.float32)
    for x in range(8):
        arrived(state_in.at[0, x], near_recv.at[3 + x])
        state[other, x, 0:SIZE_Y, :] = state_in[other, x].astype(jnp.float32)

    low_half = iota((NODES, 128), 1) < 64

    @pl.loop(0, SUBSTEPS)
    def _(step):
        few = chips // 2

        @pl.when(step < 2)
        def _():
            for k in range(1, few):
                send_forcing(step * few + k)

        @pl.when(step == 1)
        def _():
            send_forcing(few)

        @pl.when(step == 0)
        def _():
            pltpu.make_async_copy(
                forc_out.at[chip_rows(chip)], forc_in.at[core, chip_rows(chip)], forc_recv.at[0]
            ).start()

        @pl.loop(0, NODES // 8)
        def _(i):
            for face in range(2):
                for e in range(0, 8, 4):

                    def rows(j):
                        return pl.ds(i * 32 + j, 8, stride=4)

                    s = [[state[face, e + a, rows(j), :] for j in range(4)] for a in range(4)]
                    along_y = [derivative(s[a]) for a in range(4)]
                    for j in range(4):
                        along_x = derivative([s[a][j] for a in range(4)])
                        for a in range(4):
                            value = wind[0, face, e + a, rows(j), :] * along_x[a]
                            value = value + wind[1, face, e + a, rows(j), :] * along_y[a][j]
                            rate[face, e + a, j, pl.ds(pl.multiple_of(i * 8, 8), 8), :] = value

        def summed(face, x, j):
            value = rate[face, x, j]
            if x == 3:
                return value + rate[face, 4, j]
            if x == 4:
                return rate[face, 3, j] + value
            if x == 7:
                pair = jnp.where(low_half, rate[1 - face, 0, j], rate[face, 0, j])
                return value + pltpu.roll(pair, 64, 1)
            if x == 0:
                pair = jnp.where(low_half, rate[face, 7, j], rate[1 - face, 7, j])
                return value + pltpu.roll(pair, 64, 1)
            return value

        for face in range(2):
            for x in range(8):
                z = [summed(face, x, j) for j in range(4)]
                z[0], z[3] = (
                    z[0] + pltpu.roll(z[3], 1, 0),
                    z[3] + pltpu.roll(z[0], NODES - 1, 0),
                )
                for j in range(4):
                    rows = pl.ds(j, NODES, stride=4)
                    state[face, x, rows, :] = (
                        state[face, x, rows, :] + z[j] * inverse[face, x, rows, :]
                    )

    for face in range(2):
        for x in range(8):
            dyn[face, x * SIZE_Y : (x + 1) * SIZE_Y, :] = state[face, x, 0:SIZE_Y, :].astype(
                jnp.bfloat16
            )

    low_row = iota((2 * CHUNK, 128), 1) < 64

    @pl.loop(0, TILE_GROUPS)
    def _(i):
        chunks = [c for c, _, _ in chunks_of(i)]
        rows = [chunk_rows(c) for c in chunks]
        q = [
            [
                dot(
                    jnp.concatenate(
                        [place[face, r, xh * 1024 : (xh + 1) * 1024] for r in rows], axis=0
                    ),
                    dyn[face],
                )
                for xh in range(2)
            ]
            for face in range(2)
        ]
        turn = pltpu.roll(jnp.where(low_row, q[1][0], q[0][1]), 64, 1)
        packed = (jnp.where(low_row, q[0][0], q[1][1]) + turn).astype(jnp.bfloat16)
        for k in range(2):
            dyn_out[rows[k], :] = packed[k * CHUNK : (k + 1) * CHUNK, :]
        spread(i, chunks, dyn_out, dyn_in, dyn_recv.at[f * TILE_GROUPS + u_me])

    arrived(forc_in.at[core], forc_recv.at[0])
    sent.append(
        remote(
            forc_in.at[core],
            forc_in.at[core],
            forc_send.at[1],
            forc_recv.at[1],
            at(2 * chip + 1 - core),
        )
    )
    arrived(forc_in.at[1 - core], forc_recv.at[1])

    @pl.loop(0, COLUMNS // CHUNK)
    def _(i):
        cols = pl.ds(pl.multiple_of(i * CHUNK, CHUNK), CHUNK)
        half = CHUNK // 2
        blocks = []
        for k in range(0, half, per_peer):
            rows = pl.ds(pl.multiple_of(i * half + k, 16), per_peer)
            blocks += [forc_in[0, rows, :], forc_in[1, rows, :]]
        pre[:, cols] += dot(w_forc[...], jnp.concatenate(blocks, axis=0), NT)

    loads[6].wait()
    loads[7].wait()
    level_lane = iota((256, CHANNELS), 1)
    level_row = iota((256, CHANNELS), 0)

    @pl.loop(0, TILE_GROUPS)
    def _(i):
        steps = chunks_of(i)

        def arrive(u):
            for h in range(2):
                c = h * TILE_GROUPS + u
                arrived(dyn_in.at[chunk_rows(c)], dyn_recv.at[c])

        @pl.when(i != 2)
        def _():
            arrive(steps[0][2])

        @pl.when(i == 1)
        def _():
            arrive(steps[1][2])

        blocks, hidden = [], []
        for c, face, u in steps:
            halves = [dyn_in[chunk_rows(h * TILE_GROUPS + u), :] for h in range(2)]
            blocks.append(twice(*halves))
            first = w_dyn[:, pl.ds(pl.multiple_of(face * 256, 256), 256)]
            hidden.append(leaky(pre[:, chunk_rows(c)] + dot(first, blocks[-1].T)))
        hidden = twice(*hidden).astype(jnp.bfloat16)
        hidden = leaky(dot(w_mid_v[...], hidden) + twice(twice(bias_mid[...])))
        result = dot(w_out_v[...], hidden.astype(jnp.bfloat16)) + twice(twice(bias_out[...]))
        result = result.astype(jnp.bfloat16)
        for k, (c, face, u) in enumerate(steps):
            part = result[:, k * CHUNK : (k + 1) * CHUNK]
            diag_v[:, chunk_rows(c)] = part[CHANNELS:, :]
            row = level_lane // LEVELS * 16 + level_lane % 16
            row = row + level_lane // HALF % 2 * 128 + face * 64
            pick = (level_row == row).astype(jnp.bfloat16)
            change = part[0:CHANNELS, :].astype(jnp.float32).T
            value = dot(blocks[k], pick) + physics_weight * change
            back_out[chunk_rows(c), :] = value.astype(jnp.bfloat16)
        pair = [c for c, _, _ in steps]
        spread(i, pair, back_out, back_in, back_recv.at[f * TILE_GROUPS + u_me])

    diag_copy = pltpu.make_async_copy(diag_v, diagnostics, out_sem.at[0])
    diag_copy.start()

    for v in (2, 1, 3, 0):
        u = lax.rem(u_me + TILE_GROUPS - v, TILE_GROUPS)
        parts = []
        for face in range(2):
            c = face * TILE_GROUPS + u
            rows = pl.ds(pl.multiple_of(c * CHUNK, CHUNK), CHUNK)
            arrived(back_in.at[rows], back_recv.at[c])
            parts.append((back_in[rows, :], rows))
        for k in range(0, COLUMNS, 512):
            value = sum(dot(back, place[f, rows, k : k + 512], TN) for back, rows in parts)
            value = value.astype(jnp.bfloat16)
            total[:, k : k + 512] = value if v == 2 else total[:, k : k + 512] + value
    updated_copy = pltpu.make_async_copy(total, updated, out_sem.at[1])
    updated_copy.start()
    for copy in sent:
        copy.wait_send()
    away = pl.ds(0, (devices - 1) * per_peer)
    for out in (dyn_out, back_out):
        arrived(out.at[away], relay_send)
    arrived(forc_out.at[pl.ds(0, (chips - 1) * per_peer)], forc_send.at[0])
    diag_copy.wait()
    updated_copy.wait()


PIECES = 4


def finish(new, diag, updated, diagnostics, new_v, diag_v, updated_v, load_sem, out_sem):
    n, d = CHANNELS // PIECES, (OUT - CHANNELS) // PIECES // 16 * 16
    cuts = [pl.ds(k * n, n) for k in range(PIECES)]
    cuts += [pl.ds(k * d, d if k < PIECES - 1 else OUT - CHANNELS - k * d) for k in range(PIECES)]
    ends = ((new, new_v),) * PIECES + ((diag, diag_v),) * PIECES
    loads = [
        pltpu.make_async_copy(src.at[cut], dst.at[cut], load_sem.at[k])
        for k, (cut, (src, dst)) in enumerate(zip(cuts, ends))
    ]
    for copy in loads:
        copy.start()
    outs = []

    def out(src, dst):
        outs.append(pltpu.make_async_copy(src, dst, out_sem.at[len(outs)]))
        outs[-1].start()

    for k in range(PIECES):
        loads[k].wait()
        for x in range(SIZE_X):
            block = new_v[k * n : (k + 1) * n, x * SIZE_Y : (x + 1) * SIZE_Y]
            updated_v[pl.ds(k * n * SIZE_X + x, n, stride=SIZE_X), :] = block.astype(jnp.float32)
        rows = pl.ds(k * n * SIZE_X, n * SIZE_X)
        out(updated_v.at[rows], updated.at[rows])
    for k in range(PIECES, 2 * PIECES):
        loads[k].wait()
        out(diag_v.at[cuts[k]], diagnostics.at[cuts[k]])
    for copy in outs:
        copy.wait()


def local(
    tracers,
    wind_field,
    metric,
    forcing,
    aux_inputs,
    batch_pos,
    day_of_year,
    w_in,
    b_in,
    w_mid,
    b_mid,
    w_out,
    b_out,
):
    tiles = lax.axis_size("tile")
    anywhere = pl.BlockSpec(memory_space=pl.ANY)
    f32, b16 = jnp.float32, jnp.bfloat16
    dma = pltpu.SemaphoreType.DMA
    scratch = [
        pltpu.VMEM((CHANNELS * SIZE_X, SIZE_Y), f32),
        pltpu.VMEM((2 * LEVELS * SIZE_X, SIZE_Y), f32),
        pltpu.VMEM((SIZE_X, SIZE_Y), f32),
        pltpu.VMEM((12 * FORC, SIZE_X, SIZE_Y), b16),
        pltpu.VMEM((AUX, COLUMNS), b16),
        pltpu.VMEM(w_in.shape[::-1], b16),
        pltpu.VMEM(w_mid.shape, b16),
        pltpu.VMEM(w_out.shape, b16),
        pltpu.VMEM((SIZE_X, SIZE_Y), jnp.int32),
        pltpu.SMEM((1,), jnp.int32),
        pltpu.VMEM((HIDDEN,), f32),
        pltpu.VMEM((HIDDEN,), f32),
        pltpu.VMEM((OUT,), f32),
        dma((13,)),
        pltpu.VMEM((2, 8, SIZE_Y, 128), b16),
        pltpu.VMEM((2, 4, SIZE_Y, 128), b16),
        pltpu.VMEM((2, 8, SIZE_Y, 128), b16),
        pltpu.VMEM((2, 4, SIZE_Y, 128), b16),
        pltpu.VMEM((2, 2, 8, HALO, 128), b16),
        pltpu.VMEM((2, 2, 4, HALO, 128), b16),
        pltpu.VMEM((3, 2 * SIZE_X, SIZE_Y), f32),
        pltpu.VMEM((2, SIZE_X, SIZE_Y), jnp.int32),
        pltpu.VMEM((2, 8, WIDE, 128), f32),
        pltpu.VMEM((2, 2, 8, WIDE, 128), f32),
        pltpu.VMEM((2, 8, WIDE, 128), f32),
        pltpu.VMEM((2, 8, WIDE, 128), f32),
        pltpu.VMEM((2, 8, 4, NODES, 128), f32),
        pltpu.VMEM((2, COLUMNS, COLUMNS), b16),
        pltpu.VMEM((48 * SIZE_X, SIZE_Y), f32),
        pltpu.VMEM((128, COLUMNS), b16),
        pltpu.VMEM((COLUMNS // 2, 128), b16),
        pltpu.VMEM((2, COLUMNS // 2, 128), b16),
        pltpu.VMEM((2, COLUMNS // 2, 128), b16),
        pltpu.VMEM((COLUMNS, 128), b16),
        pltpu.VMEM((COLUMNS, 128), b16),
        pltpu.VMEM((COLUMNS, 128), b16),
        pltpu.VMEM((COLUMNS, 128), b16),
        pltpu.VMEM((HIDDEN, COLUMNS), f32),
        pltpu.VMEM((HIDDEN, AUX), b16),
        pltpu.VMEM((HIDDEN, 128), b16),
        pltpu.VMEM((HIDDEN, 512), b16),
        pltpu.VMEM((HIDDEN, 128), f32),
        pltpu.VMEM((HIDDEN, 128), f32),
        pltpu.VMEM((OUT, 128), f32),
        pltpu.VMEM((OUT - CHANNELS, COLUMNS), b16),
        pltpu.VMEM((CHANNELS, COLUMNS), b16),
        pltpu.SemaphoreType.REGULAR((2,)),
        dma((11,)),
        dma((11,)),
        dma((3, 2, 2)),
        dma((3, 2, 2)),
        dma,
        dma((2,)),
        dma((2,)),
        dma((2 * TILE_GROUPS,)),
        dma((2 * TILE_GROUPS,)),
        dma((2,)),
    ]
    updated, diagnostics = pl.pallas_call(
        functools.partial(kernel, tiles),
        out_shape=(
            jax.ShapeDtypeStruct((CHANNELS, COLUMNS), b16),
            jax.ShapeDtypeStruct((OUT - CHANNELS, COLUMNS), b16),
        ),
        in_specs=[anywhere] * 13,
        out_specs=(anywhere, anywhere),
        scratch_shapes=scratch,
        compiler_params=pltpu.CompilerParams(
            collective_id=0, has_side_effects=True, vmem_limit_bytes=60 * 2**20
        ),
    )(
        tracers.reshape(CHANNELS * SIZE_X, SIZE_Y),
        wind_field.reshape(2 * LEVELS * SIZE_X, SIZE_Y),
        metric,
        forcing.reshape(12 * FORC, SIZE_X, SIZE_Y),
        aux_inputs,
        batch_pos,
        day_of_year,
        w_in.T,
        b_in,
        w_mid,
        b_mid,
        w_out,
        b_out,
    )
    updated, diagnostics = pl.pallas_call(
        finish,
        out_shape=(
            jax.ShapeDtypeStruct((CHANNELS * SIZE_X, SIZE_Y), f32),
            jax.ShapeDtypeStruct((OUT - CHANNELS, COLUMNS), b16),
        ),
        in_specs=[anywhere, anywhere],
        out_specs=(anywhere, anywhere),
        scratch_shapes=[
            pltpu.VMEM((CHANNELS, COLUMNS), b16),
            pltpu.VMEM((OUT - CHANNELS, COLUMNS), b16),
            pltpu.VMEM((CHANNELS * SIZE_X, SIZE_Y), f32),
            dma((2 * PIECES,)),
            dma((2 * PIECES,)),
        ],
        compiler_params=pltpu.CompilerParams(vmem_limit_bytes=60 * 2**20),
    )(updated, diagnostics)
    return updated.reshape(tracers.shape), diagnostics


def solution(mesh):
    placed = (
        P(None, None, "face", "tile"),
        P(None, None, "face", "tile"),
        P("face", "tile"),
        P(None, None, "face", "tile"),
        P(None, ("face", "tile")),
        P("face", "tile"),
        P(),
        P(),
        P(),
        P(),
        P(),
        P(),
        P(),
    )
    return jax.shard_map(
        local,
        mesh=mesh,
        in_specs=placed,
        out_specs=(P(None, None, "face", "tile"), P(None, ("face", "tile"))),
        check_vma=False,
    )
```

```python
import functools

import jax
import jax.numpy as jnp
import numpy as np
from jax import lax
from jax.experimental import pallas as pl
from jax.experimental.pallas import tpu as pltpu
from jax.sharding import PartitionSpec as P

SUBSTEPS = 4
FIELDS = 4
LEVELS = 32
HALF = 16
SIZE_X = 16
SIZE_Y = 128
COLUMNS = SIZE_X * SIZE_Y
CHANNELS = FIELDS * LEVELS
FORC = 44
AUX = 384
HIDDEN = 512
OUT = 368
HALO = 16
WIDE = SIZE_Y + 2 * HALO
NODES = WIDE // 4
CHUNK = 256
TILE_GROUPS = 4

MESH = pl.DeviceIdType.MESH
leak_slope = 0.15
time_step = 0.05
physics_weight = 0.5

root = np.sqrt(5.0)
big = 5.0 * (root + 1.0) / 4.0
mid = 5.0 * (root - 1.0) / 4.0
near = (root + 1.0) / 4.0
far = (root - 1.0) / 4.0


def derivative(s):
    c, d = s[0] - s[3], s[1] - s[2]
    e = (s[1] + s[2]) - (s[0] + s[3])
    p = (-1.75) * c + ((big + mid) / 2.0) * d
    q = (-(near - far) / 2.0) * c - (root / 4.0) * d
    outer, inner = 1.25 * e, (root / 4.0) * e
    return [p + outer, q + inner, q - inner, p - outer]


def leaky(value):
    return jnp.where(value > 0, value, leak_slope * value)


def iota(shape, dim):
    return lax.broadcasted_iota(jnp.int32, shape, dim)


def dot(a, b, contract=((1,), (0,))):
    return lax.dot_general(a, b, (contract, ((), ())), preferred_element_type=jnp.float32)


def stage(i):
    a = (i + 1) // 2
    pair = a % 2
    return (2 - a, 1 - pair * (i - 1)), (2 - a + 2 * pair, pair * (2 - i))


NT = ((1,), (1,))
TN = ((0,), (0,))


def kernel(
    tiles,
    tracers,
    winds,
    metric,
    forcing,
    aux,
    batch_pos,
    day,
    w_in,
    b_in,
    w_mid,
    b_mid,
    w_out,
    b_out,
    updated,
    diagnostics,
    tracers_v,
    winds_v,
    metric_v,
    forcing_v,
    aux_v,
    w_in_v,
    w_mid_v,
    w_out_v,
    pos_v,
    day_v,
    b_in_v,
    b_mid_v,
    b_out_v,
    load_sem,
    half_b16,
    wind_b16,
    state_in,
    wind_in,
    halo_state,
    halo_wind,
    metric_all,
    pos_all,
    state,
    wind,
    mass,
    inverse,
    rate,
    place,
    forc_rows,
    forc_mat,
    forc_out,
    forc_in,
    dyn,
    dyn_out,
    dyn_in,
    back_out,
    back_in,
    pre,
    w_aux,
    w_forc,
    w_dyn,
    bias_in,
    bias_mid,
    bias_out,
    diag_v,
    total,
    known,
    near_send,
    near_recv,
    halo_send,
    halo_recv,
    relay_send,
    forc_send,
    forc_recv,
    dyn_recv,
    back_recv,
    out_sem,
):
    devices = 2 * tiles
    per_peer = COLUMNS // devices
    group = tiles // TILE_GROUPS
    f = lax.axis_index("face")
    t = lax.axis_index("tile")
    me = f * tiles + t
    u_me = t // group
    k_me = t % group
    right = lax.rem(t + 1, tiles)
    left = lax.rem(t + tiles - 1, tiles)
    other = 1 - f

    def at(p):
        return (p // tiles, lax.rem(p, tiles))

    def own_rows(p):
        return pl.ds(pl.multiple_of(p * per_peer, 16), per_peer)

    loads = [
        pltpu.make_async_copy(a, b, load_sem.at[i])
        for i, (a, b) in enumerate(
            (
                (winds, winds_v),
                (tracers, tracers_v),
                (metric, metric_v),
                (w_in, w_in_v),
                (aux, aux_v),
                (forcing, forcing_v),
                (w_mid, w_mid_v),
                (w_out, w_out_v),
                (batch_pos, pos_v),
                (day, day_v),
                (b_in, b_in_v),
                (b_mid, b_mid_v),
                (b_out, b_out_v),
            )
        )
    ]
    for load in loads:
        load.start()

    def signal(sem, target):
        pl.semaphore_signal(sem, inc=1, device_id=target, device_id_type=MESH)

    near_tiles = 4
    middle = min(4, tiles // near_tiles)
    high = tiles // (near_tiles * middle)
    t_low, t_middle, t_high = t % near_tiles, t // near_tiles % middle, t // (near_tiles * middle)
    along_middle = [
        t + (lax.rem(t_middle + k, middle) - t_middle) * near_tiles for k in range(1, middle)
    ]
    along_high = [
        t + (lax.rem(t_high + k, high) - t_high) * near_tiles * middle for k in range(1, high)
    ]
    along_low = [t - t_low + lax.rem(t_low + k, near_tiles) for k in range(near_tiles)]
    greeted = [(other, tile) for tile in along_low] + [(f, tile) for tile in along_low[1:]]
    greeted += [(f, tile) for tile in [right, left] + along_middle + along_high]
    barrier = pltpu.get_barrier_semaphore()
    for target in greeted:
        signal(barrier, target)

    def remote(src, dst, send, recv, target):
        copy = pltpu.make_async_remote_copy(
            src, dst, send, recv, device_id=target, device_id_type=MESH
        )
        copy.start()
        return copy

    def arrived(ref, sem):
        pltpu.make_async_copy(ref, ref, sem).wait()

    def turn_winds(h):
        for g in range(4):
            rows = [
                winds_v[pl.ds(c * 512 + h * 256 + xh * 8 + 2 * g + lo, HALF, stride=SIZE_X), :]
                for c in range(2)
                for lo in range(2)
                for xh in range(2)
            ]
            wind_b16[h, g] = jnp.concatenate(rows, axis=0).T.astype(jnp.bfloat16)

    def turn_state(h, x):
        rows = [
            tracers_v[pl.ds(i * 512 + h * 256 + xh * 8 + x, HALF, stride=SIZE_X), :]
            for xh in range(2)
            for i in range(FIELDS)
        ]
        turned = jnp.concatenate(rows, axis=0).T
        half_b16[h, x] = turned.astype(jnp.bfloat16)
        return turned

    partner = (other, t)
    loads[0].wait()
    turn_winds(other)
    loads[1].wait()
    turn_state(other, 0)
    pl.semaphore_wait(barrier, len(greeted))
    for tile in along_middle:
        signal(known.at[0], (f, tile))
    sent = [
        remote(wind_b16.at[other], wind_in.at[f], near_send.at[2], near_recv.at[2], partner)
    ]
    for x in range(8):
        if x > 0:
            turn_state(other, x)
        sent.append(
            remote(
                half_b16.at[other, x],
                state_in.at[f, x],
                near_send.at[3 + x],
                near_recv.at[3 + x],
                partner,
            )
        )
    loads[2].wait()
    loads[8].wait()
    face_rows = pl.ds(pl.multiple_of(f * SIZE_X, SIZE_X), SIZE_X)
    sent += [
        remote(metric_v, metric_all.at[0, face_rows], near_send.at[0], near_recv.at[0], partner),
        remote(pos_v, pos_all.at[f], near_send.at[1], near_recv.at[1], partner),
    ]
    metric_all[0, face_rows, :] = metric_v[...]
    pos_all[f] = pos_v[...]
    turn_winds(f)
    for x in range(8):
        state[f, x, 0:SIZE_Y, :] = turn_state(f, x)

    def send_halo(face):
        for side, tile, start in ((0, right, SIZE_Y - HALO), (1, left, 0)):
            rows = pl.ds(start, HALO)
            for kind, src, dst in (
                (0, metric_v, metric_all.at[1 + side, face_rows]),
                (1, wind_b16.at[face, :, rows], halo_wind.at[side, f]),
                (2, half_b16.at[face, :, rows], halo_state.at[side, f]),
            ):
                sent.append(
                    remote(
                        src,
                        dst,
                        halo_send.at[kind, side, face],
                        halo_recv.at[kind, side, f],
                        (face, tile),
                    )
                )

    if middle > 1:
        pl.semaphore_wait(known.at[0], middle - 1)
    for tile in along_high:
        signal(known.at[1], (f, tile))
    send_halo(f)

    def fill_place(face):
        pos = pos_all[face]
        slot = pos // COLUMNS * per_peer + pos % per_peer
        one = jnp.ones((CHUNK, SIZE_Y), jnp.bfloat16)
        zero = jnp.zeros((CHUNK, SIZE_Y), jnp.bfloat16)

        @pl.loop(0, COLUMNS // CHUNK)
        def _(i):
            rows = pl.ds(pl.multiple_of(i * CHUNK, CHUNK), CHUNK)
            index = iota((CHUNK, SIZE_Y), 0).astype(jnp.int16)
            here = slot - i * CHUNK
            for x in range(SIZE_X):
                row = jnp.broadcast_to(here[x : x + 1, :], (16, SIZE_Y)).astype(jnp.int16)
                row = jnp.concatenate([row] * (CHUNK // 16), axis=0)
                hit = jnp.where(index == row, one, zero)
                place[face, rows, x * SIZE_Y : (x + 1) * SIZE_Y] = hit

    fill_place(f)
    if high > 1:
        pl.semaphore_wait(known.at[1], high - 1)
    send_halo(other)

    loads[5].wait()
    loads[9].wait()
    months = day_v[0] * 12
    month_lo = months // 365
    month_hi = lax.rem(month_lo + 1, 12)
    part = jnp.full((1, 1, SIZE_Y), months - month_lo * 365, jnp.int32).astype(jnp.float32) / 365.0
    for c in range(0, FORC, 4):
        lower = forcing_v[pl.ds(month_lo * FORC + c, 4)].astype(jnp.float32)
        upper = forcing_v[pl.ds(month_hi * FORC + c, 4)].astype(jnp.float32)
        now = (1.0 - part) * lower + part * upper
        forc_rows[c * SIZE_X : (c + 4) * SIZE_X, :] = now.reshape(4 * SIZE_X, SIZE_Y)
    forc_rows[FORC * SIZE_X :, :] = jnp.zeros((4 * SIZE_X, SIZE_Y), jnp.float32)
    for x in range(SIZE_X):
        block = forc_rows[pl.ds(x, 48, stride=SIZE_X), :].astype(jnp.bfloat16)
        for k in (0, 64):
            forc_mat[k : k + 48, x * SIZE_Y : (x + 1) * SIZE_Y] = block
    for k in (48, 112):
        forc_mat[k : k + 16, :] = jnp.zeros((16, COLUMNS), jnp.bfloat16)

    low_size = min(near_tiles, group)
    z_size = group // low_size
    z_me = k_me // low_size
    far_first = sorted(range(group), key=lambda k: -min(k // low_size, z_size - k // low_size))

    def spread(i, pair, out, dst, recv):
        def send(c, k):
            p = c * group + (z_me + k // low_size) % z_size * low_size + (k_me + k) % low_size
            pltpu.make_async_remote_copy(
                out.at[own_rows(p)],
                dst.at[own_rows(me)],
                relay_send,
                recv,
                device_id=at(p),
                device_id_type=MESH,
            ).start()

        @pl.when(i == TILE_GROUPS - 1)
        def _():
            for k in far_first:
                send(pair[0], k)
                if k > 0:
                    send(pair[1], k)
            pltpu.make_async_copy(out.at[own_rows(me)], dst.at[own_rows(me)], recv).start()

        @pl.when(i < TILE_GROUPS - 1)
        def _():
            for k in far_first:
                for c in pair:
                    send(c, k)

    def chunks_of(i):
        found = []
        for on, away in stage(i):
            face, u = lax.rem(f + away, 2), lax.rem(u_me + on, TILE_GROUPS)
            found.append((face * TILE_GROUPS + u, face, u))
        return found

    def chunk_rows(c):
        return pl.ds(pl.multiple_of(c * CHUNK, CHUNK), CHUNK)

    chips = devices // 2
    core = lax.rem(t, 2)
    low_lane = iota((per_peer, 128), 1) < 64

    def chip_rows(g):
        return pl.ds(pl.multiple_of(g * per_peer, 16), per_peer)

    @pl.loop(0, COLUMNS // CHUNK)
    def _(i):
        n = CHUNK // per_peer
        rows = pl.ds(pl.multiple_of(i * CHUNK, CHUNK), CHUNK)
        value = dot(place[f, rows, :], forc_mat[...], NT)
        for k in range(0, max(n, 1), 2):
            both = [value[(k + m) * per_peer : (k + m + 1) * per_peer, :] for m in range(2)]
            packed = jnp.where(low_lane, both[0], both[1]).astype(jnp.bfloat16)
            forc_out[chip_rows((i * n + k) // 2), :] = packed

    chip = me // 2

    def send_forcing(k):
        g = lax.rem(chip + k, chips)
        pltpu.make_async_remote_copy(
            forc_out.at[chip_rows(g)],
            forc_in.at[core, chip_rows(chip)],
            forc_send.at[0],
            forc_recv.at[0],
            device_id=at(2 * g + core),
            device_id_type=MESH,
        ).start()

    def spread_bias(ref, into, size):
        for k in range(0, size, 128):
            n = min(128, size - k)
            into[k : k + n, :] = jnp.broadcast_to(ref[k : k + n].reshape(1, n), (128, n)).T

    for load in loads[10:]:
        load.wait()
    spread_bias(b_in_v, bias_in, HIDDEN)
    spread_bias(b_mid_v, bias_mid, HIDDEN)
    spread_bias(b_out_v, bias_out, OUT)
    loads[3].wait()
    w_aux[...] = w_in_v[CHANNELS + FORC :, :].T
    row = iota((CHANNELS, 128), 0)
    pick = (iota((CHANNELS, 128), 1) == row + core * 64) & (row < FORC)
    w_forc[...] = dot(
        w_in_v[CHANNELS : 2 * CHANNELS, :], pick.astype(jnp.bfloat16), TN
    ).astype(jnp.bfloat16)
    lane = iota((CHANNELS, 512), 1)
    ch = (lane // 16) % 4 * LEVELS + lane // 128 % 2 * HALF + lane % 16
    pick = (iota((CHANNELS, 512), 0) == ch) & (lane // 64 % 2 == lane // 256)
    w_dyn[...] = dot(w_in_v[0:CHANNELS, :], pick.astype(jnp.bfloat16), TN).astype(jnp.bfloat16)
    loads[4].wait()

    def twice(one, two=None):
        return jnp.concatenate([one, one if two is None else two], axis=1)

    @pl.loop(0, COLUMNS // CHUNK)
    def _(i):
        cols = pl.ds(pl.multiple_of(i * CHUNK, CHUNK), CHUNK)
        pre[:, cols] = dot(w_aux[...], aux_v[:, cols]) + twice(bias_in[...])

    arrived(pos_all.at[0], near_recv.at[1])
    fill_place(other)

    arrived(metric_all.at[0, pl.ds(0, SIZE_X)], near_recv.at[0])
    for face in range(2):
        for side in range(2):
            arrived(metric_all.at[1 + side, pl.ds(0, SIZE_X)], halo_recv.at[0, side, face])

    def node_weight(shape, dim):
        n = iota(shape, dim) % 4
        return jnp.where((n == 0) | (n == 3), np.float32(1.0 / 6.0), np.float32(5.0 / 6.0))

    turned = []
    for k in range(3):
        block = metric_all[k] * node_weight((32, SIZE_Y), 0) * node_weight((32, SIZE_Y), 1)
        turned.append(jnp.concatenate([block] * 4, axis=0).T)
    points = jnp.concatenate([turned[0], turned[2][:HALO], turned[1][SIZE_Y - HALO :]], axis=0)
    node_x = iota((WIDE, 128), 1) % 4
    node_y = iota((WIDE, 128), 0) % 4
    along = points + jnp.where(node_x == 0, pltpu.roll(points, 1, 1), 0.0)
    along = along + jnp.where(node_x == 3, pltpu.roll(points, 127, 1), 0.0)
    both = along + jnp.where(node_y == 0, pltpu.roll(along, 1, 0), 0.0)
    both = both + jnp.where(node_y == 3, pltpu.roll(along, WIDE - 1, 0), 0.0)
    scaled, inverted = -time_step * points, 1.0 / both
    low = iota((WIDE, 128), 1) < 64
    for face in range(2):
        for x in range(8):
            k = face * SIZE_X + x
            for value, into in ((scaled, mass), (inverted, inverse)):
                one = jnp.broadcast_to(value[:, k : k + 1], (WIDE, 128))
                two = jnp.broadcast_to(value[:, k + 8 : k + 9], (WIDE, 128))
                into[face, x] = jnp.where(low, one, two)

    wind_in[f] = wind_b16[f]
    out_lane = iota((128, 512), 1)
    from_lane = out_lane // 128 * 32 + out_lane // 64 % 2 * 16 + out_lane % 16
    widen = (iota((128, 512), 0) == from_lane).astype(jnp.bfloat16)
    for kind in (1, 2):
        for face in range(2):
            for side in range(2):
                ref = (halo_wind, halo_state)[kind - 1].at[side, face]
                arrived(ref, halo_recv.at[kind, side, face])
    arrived(wind_in.at[0], near_recv.at[2])
    for face in range(2):
        for g in range(4):
            rows = jnp.concatenate(
                [wind_in[face, g], halo_wind[1, face, g], halo_wind[0, face, g]], axis=0
            )
            wide = dot(rows, widen)
            for c in range(2):
                for lo in range(2):
                    k = 2 * c + lo
                    x = 2 * g + lo
                    wind[c, face, x] = wide[:, k * 128 : (k + 1) * 128] * mass[face, x]
    for face in range(2):
        state[face, :, SIZE_Y : SIZE_Y + HALO, :] = halo_state[1, face].astype(jnp.float32)
        state[face, :, SIZE_Y + HALO :, :] = halo_state[0, face].astype(jnp.float32)
    for x in range(8):
        arrived(state_in.at[0, x], near_recv.at[3 + x])
        state[other, x, 0:SIZE_Y, :] = state_in[other, x].astype(jnp.float32)

    low_half = iota((NODES, 128), 1) < 64

    @pl.loop(0, SUBSTEPS)
    def _(step):
        @pl.when(step == 0)
        def _():
            for k in range(1, chips):
                send_forcing(k)

        @pl.when(step == 0)
        def _():
            pltpu.make_async_copy(
                forc_out.at[chip_rows(chip)], forc_in.at[core, chip_rows(chip)], forc_recv.at[0]
            ).start()

        @pl.loop(0, NODES // 8)
        def _(i):
            for face in range(2):
                for e in range(0, 8, 4):

                    def rows(j):
                        return pl.ds(i * 32 + j, 8, stride=4)

                    s = [[state[face, e + a, rows(j), :] for j in range(4)] for a in range(4)]
                    along_y = [derivative(s[a]) for a in range(4)]
                    for j in range(4):
                        along_x = derivative([s[a][j] for a in range(4)])
                        for a in range(4):
                            value = wind[0, face, e + a, rows(j), :] * along_x[a]
                            value = value + wind[1, face, e + a, rows(j), :] * along_y[a][j]
                            rate[face, e + a, j, pl.ds(pl.multiple_of(i * 8, 8), 8), :] = value

        def summed(face, x, j):
            value = rate[face, x, j]
            if x == 3:
                return value + rate[face, 4, j]
            if x == 4:
                return rate[face, 3, j] + value
            if x == 7:
                pair = jnp.where(low_half, rate[1 - face, 0, j], rate[face, 0, j])
                return value + pltpu.roll(pair, 64, 1)
            if x == 0:
                pair = jnp.where(low_half, rate[face, 7, j], rate[1 - face, 7, j])
                return value + pltpu.roll(pair, 64, 1)
            return value

        for face in range(2):
            for x in range(8):
                z = [summed(face, x, j) for j in range(4)]
                z[0], z[3] = (
                    z[0] + pltpu.roll(z[3], 1, 0),
                    z[3] + pltpu.roll(z[0], NODES - 1, 0),
                )
                for j in range(4):
                    rows = pl.ds(j, NODES, stride=4)
                    state[face, x, rows, :] = (
                        state[face, x, rows, :] + z[j] * inverse[face, x, rows, :]
                    )

    for face in range(2):
        for x in range(8):
            dyn[face, x * SIZE_Y : (x + 1) * SIZE_Y, :] = state[face, x, 0:SIZE_Y, :].astype(
                jnp.bfloat16
            )

    low_row = iota((2 * CHUNK, 128), 1) < 64

    @pl.loop(0, TILE_GROUPS)
    def _(i):
        @pl.when(i == TILE_GROUPS - 2)
        def _():
            arrived(forc_in.at[core], forc_recv.at[0])
            remote(
                forc_in.at[core],
                forc_in.at[core],
                forc_send.at[1],
                forc_recv.at[1],
                at(2 * chip + 1 - core),
            )

        chunks = [c for c, _, _ in chunks_of(i)]
        rows = [chunk_rows(c) for c in chunks]
        q = [
            [
                dot(
                    jnp.concatenate(
                        [place[face, r, xh * 1024 : (xh + 1) * 1024] for r in rows], axis=0
                    ),
                    dyn[face],
                )
                for xh in range(2)
            ]
            for face in range(2)
        ]
        turn = pltpu.roll(jnp.where(low_row, q[1][0], q[0][1]), 64, 1)
        packed = (jnp.where(low_row, q[0][0], q[1][1]) + turn).astype(jnp.bfloat16)
        for k in range(2):
            dyn_out[rows[k], :] = packed[k * CHUNK : (k + 1) * CHUNK, :]
        spread(i, chunks, dyn_out, dyn_in, dyn_recv.at[f * TILE_GROUPS + u_me])

    arrived(forc_in.at[1 - core], forc_recv.at[1])

    @pl.loop(0, COLUMNS // CHUNK // 2)
    def _(i):
        cols = pl.ds(pl.multiple_of(i * 2 * CHUNK, 2 * CHUNK), 2 * CHUNK)
        half = CHUNK
        blocks = []
        for k in range(0, half, per_peer):
            rows = pl.ds(pl.multiple_of(i * half + k, 16), per_peer)
            blocks += [forc_in[0, rows, :], forc_in[1, rows, :]]
        pre[:, cols] += dot(w_forc[...], jnp.concatenate(blocks, axis=0), NT)

    loads[6].wait()
    loads[7].wait()
    level_lane = iota((256, CHANNELS), 1)
    level_row = iota((256, CHANNELS), 0)

    @pl.loop(0, TILE_GROUPS)
    def _(i):
        steps = chunks_of(i)

        def arrive(u):
            for h in range(2):
                c = h * TILE_GROUPS + u
                arrived(dyn_in.at[chunk_rows(c)], dyn_recv.at[c])

        @pl.when(i != 2)
        def _():
            arrive(steps[0][2])

        @pl.when(i == 1)
        def _():
            arrive(steps[1][2])

        blocks, hidden = [], []
        for c, face, u in steps:
            halves = [dyn_in[chunk_rows(h * TILE_GROUPS + u), :] for h in range(2)]
            blocks.append(twice(*halves))
            first = w_dyn[:, pl.ds(pl.multiple_of(face * 256, 256), 256)]
            hidden.append(leaky(pre[:, chunk_rows(c)] + dot(first, blocks[-1].T)))
        hidden = twice(*hidden).astype(jnp.bfloat16)
        hidden = leaky(dot(w_mid_v[...], hidden) + twice(twice(bias_mid[...])))
        result = dot(w_out_v[...], hidden.astype(jnp.bfloat16)) + twice(twice(bias_out[...]))
        result = result.astype(jnp.bfloat16)
        for k, (c, face, u) in enumerate(steps):
            part = result[:, k * CHUNK : (k + 1) * CHUNK]
            diag_v[:, chunk_rows(c)] = part[CHANNELS:, :]
            row = level_lane // LEVELS * 16 + level_lane % 16
            row = row + level_lane // HALF % 2 * 128 + face * 64
            pick = (level_row == row).astype(jnp.bfloat16)
            change = part[0:CHANNELS, :].astype(jnp.float32).T
            value = dot(blocks[k], pick) + physics_weight * change
            back_out[chunk_rows(c), :] = value.astype(jnp.bfloat16)
        pair = [c for c, _, _ in steps]
        spread(i, pair, back_out, back_in, back_recv.at[f * TILE_GROUPS + u_me])

    diag_copy = pltpu.make_async_copy(diag_v, diagnostics, out_sem.at[0])
    diag_copy.start()

    for v in (2, 1, 3, 0):
        u = lax.rem(u_me + TILE_GROUPS - v, TILE_GROUPS)
        parts = []
        for face in range(2):
            c = face * TILE_GROUPS + u
            rows = pl.ds(pl.multiple_of(c * CHUNK, CHUNK), CHUNK)
            arrived(back_in.at[rows], back_recv.at[c])
            parts.append((back_in[rows, :], rows))
        for k in range(0, COLUMNS, 512):
            value = sum(dot(back, place[f, rows, k : k + 512], TN) for back, rows in parts)
            value = value.astype(jnp.bfloat16)
            total[:, k : k + 512] = value if v == 2 else total[:, k : k + 512] + value
    updated_copy = pltpu.make_async_copy(total, updated, out_sem.at[1])
    updated_copy.start()
    for copy in sent:
        copy.wait_send()
    away = pl.ds(0, (devices - 1) * per_peer)
    for out in (dyn_out, back_out):
        arrived(out.at[away], relay_send)
    arrived(forc_out.at[pl.ds(0, (chips - 1) * per_peer)], forc_send.at[0])
    arrived(forc_in.at[core], forc_send.at[1])
    diag_copy.wait()
    updated_copy.wait()


PIECES = 4


def finish(new, diag, updated, diagnostics, new_v, diag_v, updated_v, load_sem, out_sem):
    n, d = CHANNELS // PIECES, (OUT - CHANNELS) // PIECES // 16 * 16
    cuts = [pl.ds(k * n, n) for k in range(PIECES)]
    cuts += [pl.ds(k * d, d if k < PIECES - 1 else OUT - CHANNELS - k * d) for k in range(PIECES)]
    ends = ((new, new_v),) * PIECES + ((diag, diag_v),) * PIECES
    loads = [
        pltpu.make_async_copy(src.at[cut], dst.at[cut], load_sem.at[k])
        for k, (cut, (src, dst)) in enumerate(zip(cuts, ends))
    ]
    for copy in loads:
        copy.start()
    outs = []

    def out(src, dst):
        outs.append(pltpu.make_async_copy(src, dst, out_sem.at[len(outs)]))
        outs[-1].start()

    for k in range(PIECES):
        loads[k].wait()
        for x in range(SIZE_X):
            block = new_v[k * n : (k + 1) * n, x * SIZE_Y : (x + 1) * SIZE_Y]
            updated_v[pl.ds(k * n * SIZE_X + x, n, stride=SIZE_X), :] = block.astype(jnp.float32)
        rows = pl.ds(k * n * SIZE_X, n * SIZE_X)
        out(updated_v.at[rows], updated.at[rows])
    for k in range(PIECES, 2 * PIECES):
        loads[k].wait()
        out(diag_v.at[cuts[k]], diagnostics.at[cuts[k]])
    for copy in outs:
        copy.wait()


def local(
    tracers,
    wind_field,
    metric,
    forcing,
    aux_inputs,
    batch_pos,
    day_of_year,
    w_in,
    b_in,
    w_mid,
    b_mid,
    w_out,
    b_out,
):
    tiles = lax.axis_size("tile")
    anywhere = pl.BlockSpec(memory_space=pl.ANY)
    f32, b16 = jnp.float32, jnp.bfloat16
    dma = pltpu.SemaphoreType.DMA
    scratch = [
        pltpu.VMEM((CHANNELS * SIZE_X, SIZE_Y), f32),
        pltpu.VMEM((2 * LEVELS * SIZE_X, SIZE_Y), f32),
        pltpu.VMEM((SIZE_X, SIZE_Y), f32),
        pltpu.VMEM((12 * FORC, SIZE_X, SIZE_Y), b16),
        pltpu.VMEM((AUX, COLUMNS), b16),
        pltpu.VMEM(w_in.shape[::-1], b16),
        pltpu.VMEM(w_mid.shape, b16),
        pltpu.VMEM(w_out.shape, b16),
        pltpu.VMEM((SIZE_X, SIZE_Y), jnp.int32),
        pltpu.SMEM((1,), jnp.int32),
        pltpu.VMEM((HIDDEN,), f32),
        pltpu.VMEM((HIDDEN,), f32),
        pltpu.VMEM((OUT,), f32),
        dma((13,)),
        pltpu.VMEM((2, 8, SIZE_Y, 128), b16),
        pltpu.VMEM((2, 4, SIZE_Y, 128), b16),
        pltpu.VMEM((2, 8, SIZE_Y, 128), b16),
        pltpu.VMEM((2, 4, SIZE_Y, 128), b16),
        pltpu.VMEM((2, 2, 8, HALO, 128), b16),
        pltpu.VMEM((2, 2, 4, HALO, 128), b16),
        pltpu.VMEM((3, 2 * SIZE_X, SIZE_Y), f32),
        pltpu.VMEM((2, SIZE_X, SIZE_Y), jnp.int32),
        pltpu.VMEM((2, 8, WIDE, 128), f32),
        pltpu.VMEM((2, 2, 8, WIDE, 128), f32),
        pltpu.VMEM((2, 8, WIDE, 128), f32),
        pltpu.VMEM((2, 8, WIDE, 128), f32),
        pltpu.VMEM((2, 8, 4, NODES, 128), f32),
        pltpu.VMEM((2, COLUMNS, COLUMNS), b16),
        pltpu.VMEM((48 * SIZE_X, SIZE_Y), f32),
        pltpu.VMEM((128, COLUMNS), b16),
        pltpu.VMEM((COLUMNS // 2, 128), b16),
        pltpu.VMEM((2, COLUMNS // 2, 128), b16),
        pltpu.VMEM((2, COLUMNS // 2, 128), b16),
        pltpu.VMEM((COLUMNS, 128), b16),
        pltpu.VMEM((COLUMNS, 128), b16),
        pltpu.VMEM((COLUMNS, 128), b16),
        pltpu.VMEM((COLUMNS, 128), b16),
        pltpu.VMEM((HIDDEN, COLUMNS), f32),
        pltpu.VMEM((HIDDEN, AUX), b16),
        pltpu.VMEM((HIDDEN, 128), b16),
        pltpu.VMEM((HIDDEN, 512), b16),
        pltpu.VMEM((HIDDEN, 128), f32),
        pltpu.VMEM((HIDDEN, 128), f32),
        pltpu.VMEM((OUT, 128), f32),
        pltpu.VMEM((OUT - CHANNELS, COLUMNS), b16),
        pltpu.VMEM((CHANNELS, COLUMNS), b16),
        pltpu.SemaphoreType.REGULAR((2,)),
        dma((11,)),
        dma((11,)),
        dma((3, 2, 2)),
        dma((3, 2, 2)),
        dma,
        dma((2,)),
        dma((2,)),
        dma((2 * TILE_GROUPS,)),
        dma((2 * TILE_GROUPS,)),
        dma((2,)),
    ]
    updated, diagnostics = pl.pallas_call(
        functools.partial(kernel, tiles),
        out_shape=(
            jax.ShapeDtypeStruct((CHANNELS, COLUMNS), b16),
            jax.ShapeDtypeStruct((OUT - CHANNELS, COLUMNS), b16),
        ),
        in_specs=[anywhere] * 13,
        out_specs=(anywhere, anywhere),
        scratch_shapes=scratch,
        compiler_params=pltpu.CompilerParams(
            collective_id=0, has_side_effects=True, vmem_limit_bytes=60 * 2**20
        ),
    )(
        tracers.reshape(CHANNELS * SIZE_X, SIZE_Y),
        wind_field.reshape(2 * LEVELS * SIZE_X, SIZE_Y),
        metric,
        forcing.reshape(12 * FORC, SIZE_X, SIZE_Y),
        aux_inputs,
        batch_pos,
        day_of_year,
        w_in.T,
        b_in,
        w_mid,
        b_mid,
        w_out,
        b_out,
    )
    updated, diagnostics = pl.pallas_call(
        finish,
        out_shape=(
            jax.ShapeDtypeStruct((CHANNELS * SIZE_X, SIZE_Y), f32),
            jax.ShapeDtypeStruct((OUT - CHANNELS, COLUMNS), b16),
        ),
        in_specs=[anywhere, anywhere],
        out_specs=(anywhere, anywhere),
        scratch_shapes=[
            pltpu.VMEM((CHANNELS, COLUMNS), b16),
            pltpu.VMEM((OUT - CHANNELS, COLUMNS), b16),
            pltpu.VMEM((CHANNELS * SIZE_X, SIZE_Y), f32),
            dma((2 * PIECES,)),
            dma((2 * PIECES,)),
        ],
        compiler_params=pltpu.CompilerParams(vmem_limit_bytes=60 * 2**20),
    )(updated, diagnostics)
    return updated.reshape(tracers.shape), diagnostics


def solution(mesh):
    placed = (
        P(None, None, "face", "tile"),
        P(None, None, "face", "tile"),
        P("face", "tile"),
        P(None, None, "face", "tile"),
        P(None, ("face", "tile")),
        P("face", "tile"),
        P(),
        P(),
        P(),
        P(),
        P(),
        P(),
        P(),
    )
    return jax.shard_map(
        local,
        mesh=mesh,
        in_specs=placed,
        out_specs=(P(None, None, "face", "tile"), P(None, ("face", "tile"))),
        check_vma=False,
    )
```

```python
import functools

import jax
import jax.numpy as jnp
import numpy as np
from jax import lax
from jax.experimental import pallas as pl
from jax.experimental.pallas import tpu as pltpu
from jax.sharding import PartitionSpec as P

SUBSTEPS = 4
FIELDS = 4
LEVELS = 32
HALF = 16
SIZE_X = 16
SIZE_Y = 128
COLUMNS = SIZE_X * SIZE_Y
CHANNELS = FIELDS * LEVELS
FORC = 44
AUX = 384
HIDDEN = 512
OUT = 368
HALO = 16
WIDE = SIZE_Y + 2 * HALO
NODES = WIDE // 4
CHUNK = 256
TILE_GROUPS = 4

MESH = pl.DeviceIdType.MESH
leak_slope = 0.15
time_step = 0.05
physics_weight = 0.5

root = np.sqrt(5.0)
big = 5.0 * (root + 1.0) / 4.0
mid = 5.0 * (root - 1.0) / 4.0
near = (root + 1.0) / 4.0
far = (root - 1.0) / 4.0


def derivative(s):
    c, d = s[0] - s[3], s[1] - s[2]
    e = (s[1] + s[2]) - (s[0] + s[3])
    p = (-1.75) * c + ((big + mid) / 2.0) * d
    q = (-(near - far) / 2.0) * c - (root / 4.0) * d
    outer, inner = 1.25 * e, (root / 4.0) * e
    return [p + outer, q + inner, q - inner, p - outer]


def leaky(value):
    return jnp.maximum(value, leak_slope * value)


def iota(shape, dim):
    return lax.broadcasted_iota(jnp.int32, shape, dim)


def dot(a, b, contract=((1,), (0,))):
    return lax.dot_general(a, b, (contract, ((), ())), preferred_element_type=jnp.float32)


def stage(i):
    a = (i + 1) // 2
    pair = a % 2
    return (2 - a, 1 - pair * (i - 1)), (2 - a + 2 * pair, pair * (2 - i))


NT = ((1,), (1,))
TN = ((0,), (0,))


def kernel(
    tiles,
    tracers,
    winds,
    metric,
    forcing,
    aux,
    batch_pos,
    day,
    w_in,
    b_in,
    w_mid,
    b_mid,
    w_out,
    b_out,
    updated,
    diagnostics,
    tracers_v,
    winds_v,
    metric_v,
    forcing_v,
    aux_v,
    w_in_v,
    w_mid_v,
    w_out_v,
    pos_v,
    day_v,
    b_in_v,
    b_mid_v,
    b_out_v,
    load_sem,
    half_b16,
    wind_b16,
    state_in,
    wind_in,
    halo_state,
    halo_wind,
    metric_all,
    pos_all,
    state,
    wind,
    mass,
    inverse,
    rate,
    place,
    forc_rows,
    forc_mat,
    forc_out,
    forc_in,
    dyn,
    dyn_out,
    dyn_in,
    back_out,
    back_in,
    pre,
    w_aux,
    w_forc,
    w_dyn,
    bias_in,
    bias_mid,
    bias_out,
    diag_v,
    total,
    known,
    near_send,
    near_recv,
    halo_send,
    halo_recv,
    relay_send,
    forc_send,
    forc_recv,
    dyn_recv,
    back_recv,
    out_sem,
):
    devices = 2 * tiles
    per_peer = COLUMNS // devices
    group = tiles // TILE_GROUPS
    f = lax.axis_index("face")
    t = lax.axis_index("tile")
    me = f * tiles + t
    u_me = t // group
    k_me = t % group
    right = lax.rem(t + 1, tiles)
    left = lax.rem(t + tiles - 1, tiles)
    other = 1 - f

    def at(p):
        return (p // tiles, lax.rem(p, tiles))

    def own_rows(p):
        return pl.ds(pl.multiple_of(p * per_peer, 16), per_peer)

    loads = [
        pltpu.make_async_copy(a, b, load_sem.at[i])
        for i, (a, b) in enumerate(
            (
                (winds, winds_v),
                (tracers, tracers_v),
                (metric, metric_v),
                (w_in, w_in_v),
                (aux, aux_v),
                (forcing, forcing_v),
                (w_mid, w_mid_v),
                (w_out, w_out_v),
                (batch_pos, pos_v),
                (day, day_v),
                (b_in, b_in_v),
                (b_mid, b_mid_v),
                (b_out, b_out_v),
            )
        )
    ]
    for load in loads:
        load.start()

    def signal(sem, target):
        pl.semaphore_signal(sem, inc=1, device_id=target, device_id_type=MESH)

    near_tiles = 4
    middle = min(4, tiles // near_tiles)
    high = tiles // (near_tiles * middle)
    t_low, t_middle, t_high = t % near_tiles, t // near_tiles % middle, t // (near_tiles * middle)
    along_middle = [
        t + (lax.rem(t_middle + k, middle) - t_middle) * near_tiles for k in range(1, middle)
    ]
    along_high = [
        t + (lax.rem(t_high + k, high) - t_high) * near_tiles * middle for k in range(1, high)
    ]
    along_low = [t - t_low + lax.rem(t_low + k, near_tiles) for k in range(near_tiles)]
    greeted = [(other, tile) for tile in along_low] + [(f, tile) for tile in along_low[1:]]
    greeted += [(f, tile) for tile in [right, left] + along_middle + along_high]
    barrier = pltpu.get_barrier_semaphore()
    for target in greeted:
        signal(barrier, target)

    def remote(src, dst, send, recv, target):
        copy = pltpu.make_async_remote_copy(
            src, dst, send, recv, device_id=target, device_id_type=MESH
        )
        copy.start()
        return copy

    def arrived(ref, sem):
        pltpu.make_async_copy(ref, ref, sem).wait()

    def turn_winds(h):
        for g in range(4):
            rows = [
                winds_v[pl.ds(c * 512 + h * 256 + xh * 8 + 2 * g + lo, HALF, stride=SIZE_X), :]
                for c in range(2)
                for lo in range(2)
                for xh in range(2)
            ]
            wind_b16[h, g] = jnp.concatenate(rows, axis=0).T.astype(jnp.bfloat16)

    def turn_state(h, x):
        rows = [
            tracers_v[pl.ds(i * 512 + h * 256 + xh * 8 + x, HALF, stride=SIZE_X), :]
            for xh in range(2)
            for i in range(FIELDS)
        ]
        turned = jnp.concatenate(rows, axis=0).T
        half_b16[h, x] = turned.astype(jnp.bfloat16)
        return turned

    partner = (other, t)
    loads[0].wait()
    turn_winds(other)
    loads[1].wait()
    turn_state(other, 0)
    pl.semaphore_wait(barrier, len(greeted))
    for tile in along_middle:
        signal(known.at[0], (f, tile))
    sent = [
        remote(wind_b16.at[other], wind_in.at[f], near_send.at[2], near_recv.at[2], partner)
    ]
    for x in range(8):
        if x > 0:
            turn_state(other, x)
        sent.append(
            remote(
                half_b16.at[other, x],
                state_in.at[f, x],
                near_send.at[3 + x],
                near_recv.at[3 + x],
                partner,
            )
        )
    loads[2].wait()
    loads[8].wait()
    face_rows = pl.ds(pl.multiple_of(f * SIZE_X, SIZE_X), SIZE_X)
    sent += [
        remote(metric_v, metric_all.at[0, face_rows], near_send.at[0], near_recv.at[0], partner),
        remote(pos_v, pos_all.at[f], near_send.at[1], near_recv.at[1], partner),
    ]
    metric_all[0, face_rows, :] = metric_v[...]
    pos_all[f] = pos_v[...]
    turn_winds(f)
    for x in range(8):
        state[f, x, 0:SIZE_Y, :] = turn_state(f, x)

    def send_halo(face):
        for side, tile, start in ((0, right, SIZE_Y - HALO), (1, left, 0)):
            rows = pl.ds(start, HALO)
            for kind, src, dst in (
                (0, metric_v, metric_all.at[1 + side, face_rows]),
                (1, wind_b16.at[face, :, rows], halo_wind.at[side, f]),
                (2, half_b16.at[face, :, rows], halo_state.at[side, f]),
            ):
                sent.append(
                    remote(
                        src,
                        dst,
                        halo_send.at[kind, side, face],
                        halo_recv.at[kind, side, f],
                        (face, tile),
                    )
                )

    if middle > 1:
        pl.semaphore_wait(known.at[0], middle - 1)
    for tile in along_high:
        signal(known.at[1], (f, tile))
    send_halo(f)

    def fill_place(face):
        pos = pos_all[face]
        slot = pos // COLUMNS * per_peer + pos % per_peer
        one = jnp.ones((CHUNK, SIZE_Y), jnp.bfloat16)
        zero = jnp.zeros((CHUNK, SIZE_Y), jnp.bfloat16)

        @pl.loop(0, COLUMNS // CHUNK)
        def _(i):
            rows = pl.ds(pl.multiple_of(i * CHUNK, CHUNK), CHUNK)
            index = iota((CHUNK, SIZE_Y), 0).astype(jnp.int16)
            here = slot - i * CHUNK
            for x in range(SIZE_X):
                row = jnp.broadcast_to(here[x : x + 1, :], (16, SIZE_Y)).astype(jnp.int16)
                row = jnp.concatenate([row] * (CHUNK // 16), axis=0)
                hit = jnp.where(index == row, one, zero)
                place[face, rows, x * SIZE_Y : (x + 1) * SIZE_Y] = hit

    fill_place(f)
    if high > 1:
        pl.semaphore_wait(known.at[1], high - 1)
    send_halo(other)

    loads[5].wait()
    loads[9].wait()
    months = day_v[0] * 12
    month_lo = months // 365
    month_hi = lax.rem(month_lo + 1, 12)
    part = jnp.full((1, 1, SIZE_Y), months - month_lo * 365, jnp.int32).astype(jnp.float32) / 365.0
    for c in range(0, FORC, 4):
        lower = forcing_v[pl.ds(month_lo * FORC + c, 4)].astype(jnp.float32)
        upper = forcing_v[pl.ds(month_hi * FORC + c, 4)].astype(jnp.float32)
        now = (1.0 - part) * lower + part * upper
        forc_rows[c * SIZE_X : (c + 4) * SIZE_X, :] = now.reshape(4 * SIZE_X, SIZE_Y)
    forc_rows[FORC * SIZE_X :, :] = jnp.zeros((4 * SIZE_X, SIZE_Y), jnp.float32)
    for x in range(SIZE_X):
        block = forc_rows[pl.ds(x, 48, stride=SIZE_X), :].astype(jnp.bfloat16)
        for k in (0, 64):
            forc_mat[k : k + 48, x * SIZE_Y : (x + 1) * SIZE_Y] = block
    for k in (48, 112):
        forc_mat[k : k + 16, :] = jnp.zeros((16, COLUMNS), jnp.bfloat16)

    low_size = min(near_tiles, group)
    z_size = group // low_size
    z_me = k_me // low_size
    far_first = sorted(range(group), key=lambda k: -min(k // low_size, z_size - k // low_size))

    def spread(i, pair, out, dst, recv):
        def send(c, k):
            p = c * group + (z_me + k // low_size) % z_size * low_size + (k_me + k) % low_size
            pltpu.make_async_remote_copy(
                out.at[own_rows(p)],
                dst.at[own_rows(me)],
                relay_send,
                recv,
                device_id=at(p),
                device_id_type=MESH,
            ).start()

        @pl.when(i == TILE_GROUPS - 1)
        def _():
            for k in far_first:
                send(pair[0], k)
                if k > 0:
                    send(pair[1], k)
            pltpu.make_async_copy(out.at[own_rows(me)], dst.at[own_rows(me)], recv).start()

        @pl.when(i < TILE_GROUPS - 1)
        def _():
            for k in far_first:
                for c in pair:
                    send(c, k)

    def chunks_of(i):
        found = []
        for on, away in stage(i):
            face, u = lax.rem(f + away, 2), lax.rem(u_me + on, TILE_GROUPS)
            found.append((face * TILE_GROUPS + u, face, u))
        return found

    def chunk_rows(c):
        return pl.ds(pl.multiple_of(c * CHUNK, CHUNK), CHUNK)

    chips = devices // 2
    core = lax.rem(t, 2)
    low_lane = iota((per_peer, 128), 1) < 64

    def chip_rows(g):
        return pl.ds(pl.multiple_of(g * per_peer, 16), per_peer)

    @pl.loop(0, COLUMNS // CHUNK)
    def _(i):
        n = CHUNK // per_peer
        rows = pl.ds(pl.multiple_of(i * CHUNK, CHUNK), CHUNK)
        value = dot(place[f, rows, :], forc_mat[...], NT)
        for k in range(0, max(n, 1), 2):
            both = [value[(k + m) * per_peer : (k + m + 1) * per_peer, :] for m in range(2)]
            packed = jnp.where(low_lane, both[0], both[1]).astype(jnp.bfloat16)
            forc_out[chip_rows((i * n + k) // 2), :] = packed

    chip = me // 2

    def send_forcing(k):
        g = lax.rem(chip + k, chips)
        pltpu.make_async_remote_copy(
            forc_out.at[chip_rows(g)],
            forc_in.at[core, chip_rows(chip)],
            forc_send.at[0],
            forc_recv.at[0],
            device_id=at(2 * g + core),
            device_id_type=MESH,
        ).start()

    def spread_bias(ref, into, size):
        for k in range(0, size, 128):
            n = min(128, size - k)
            into[k : k + n, :] = jnp.broadcast_to(ref[k : k + n].reshape(1, n), (128, n)).T

    for load in loads[10:]:
        load.wait()
    spread_bias(b_in_v, bias_in, HIDDEN)
    spread_bias(b_mid_v, bias_mid, HIDDEN)
    spread_bias(b_out_v, bias_out, OUT)
    loads[3].wait()
    w_aux[...] = w_in_v[CHANNELS + FORC :, :].T
    row = iota((CHANNELS, 128), 0)
    pick = (iota((CHANNELS, 128), 1) == row + core * 64) & (row < FORC)
    w_forc[...] = dot(
        w_in_v[CHANNELS : 2 * CHANNELS, :], pick.astype(jnp.bfloat16), TN
    ).astype(jnp.bfloat16)
    lane = iota((CHANNELS, 512), 1)
    ch = (lane // 16) % 4 * LEVELS + lane // 128 % 2 * HALF + lane % 16
    pick = (iota((CHANNELS, 512), 0) == ch) & (lane // 64 % 2 == lane // 256)
    w_dyn[...] = dot(w_in_v[0:CHANNELS, :], pick.astype(jnp.bfloat16), TN).astype(jnp.bfloat16)
    loads[4].wait()

    def twice(one, two=None):
        return jnp.concatenate([one, one if two is None else two], axis=1)

    @pl.loop(0, COLUMNS // CHUNK)
    def _(i):
        cols = pl.ds(pl.multiple_of(i * CHUNK, CHUNK), CHUNK)
        pre[:, cols] = dot(w_aux[...], aux_v[:, cols]) + twice(bias_in[...])

    arrived(pos_all.at[0], near_recv.at[1])
    fill_place(other)

    arrived(metric_all.at[0, pl.ds(0, SIZE_X)], near_recv.at[0])
    for face in range(2):
        for side in range(2):
            arrived(metric_all.at[1 + side, pl.ds(0, SIZE_X)], halo_recv.at[0, side, face])

    def node_weight(shape, dim):
        n = iota(shape, dim) % 4
        return jnp.where((n == 0) | (n == 3), np.float32(1.0 / 6.0), np.float32(5.0 / 6.0))

    turned = []
    for k in range(3):
        block = metric_all[k] * node_weight((32, SIZE_Y), 0) * node_weight((32, SIZE_Y), 1)
        turned.append(jnp.concatenate([block] * 4, axis=0).T)
    points = jnp.concatenate([turned[0], turned[2][:HALO], turned[1][SIZE_Y - HALO :]], axis=0)
    node_x = iota((WIDE, 128), 1) % 4
    node_y = iota((WIDE, 128), 0) % 4
    along = points + jnp.where(node_x == 0, pltpu.roll(points, 1, 1), 0.0)
    along = along + jnp.where(node_x == 3, pltpu.roll(points, 127, 1), 0.0)
    both = along + jnp.where(node_y == 0, pltpu.roll(along, 1, 0), 0.0)
    both = both + jnp.where(node_y == 3, pltpu.roll(along, WIDE - 1, 0), 0.0)
    scaled, inverted = -time_step * points, 1.0 / both
    low = iota((WIDE, 128), 1) < 64
    for face in range(2):
        for x in range(8):
            k = face * SIZE_X + x
            for value, into in ((scaled, mass), (inverted, inverse)):
                one = jnp.broadcast_to(value[:, k : k + 1], (WIDE, 128))
                two = jnp.broadcast_to(value[:, k + 8 : k + 9], (WIDE, 128))
                into[face, x] = jnp.where(low, one, two)

    wind_in[f] = wind_b16[f]
    out_lane = iota((128, 512), 1)
    from_lane = out_lane // 128 * 32 + out_lane // 64 % 2 * 16 + out_lane % 16
    widen = (iota((128, 512), 0) == from_lane).astype(jnp.bfloat16)
    for kind in (1, 2):
        for face in range(2):
            for side in range(2):
                ref = (halo_wind, halo_state)[kind - 1].at[side, face]
                arrived(ref, halo_recv.at[kind, side, face])
    arrived(wind_in.at[0], near_recv.at[2])
    for face in range(2):
        for g in range(4):
            rows = jnp.concatenate(
                [wind_in[face, g], halo_wind[1, face, g], halo_wind[0, face, g]], axis=0
            )
            wide = dot(rows, widen)
            for c in range(2):
                for lo in range(2):
                    k = 2 * c + lo
                    x = 2 * g + lo
                    wind[c, face, x] = wide[:, k * 128 : (k + 1) * 128] * mass[face, x]
    for face in range(2):
        state[face, :, SIZE_Y : SIZE_Y + HALO, :] = halo_state[1, face].astype(jnp.float32)
        state[face, :, SIZE_Y + HALO :, :] = halo_state[0, face].astype(jnp.float32)
    for x in range(8):
        arrived(state_in.at[0, x], near_recv.at[3 + x])
        state[other, x, 0:SIZE_Y, :] = state_in[other, x].astype(jnp.float32)

    low_half = iota((NODES, 128), 1) < 64

    @pl.loop(0, SUBSTEPS)
    def _(step):
        @pl.when(step == 0)
        def _():
            for k in range(1, chips):
                send_forcing(k)

        @pl.when(step == 0)
        def _():
            pltpu.make_async_copy(
                forc_out.at[chip_rows(chip)], forc_in.at[core, chip_rows(chip)], forc_recv.at[0]
            ).start()

        @pl.loop(0, NODES // 8)
        def _(i):
            for face in range(2):
                for e in range(0, 8, 4):

                    def rows(j):
                        return pl.ds(i * 32 + j, 8, stride=4)

                    s = [[state[face, e + a, rows(j), :] for j in range(4)] for a in range(4)]
                    along_y = [derivative(s[a]) for a in range(4)]
                    for j in range(4):
                        along_x = derivative([s[a][j] for a in range(4)])
                        for a in range(4):
                            value = wind[0, face, e + a, rows(j), :] * along_x[a]
                            value = value + wind[1, face, e + a, rows(j), :] * along_y[a][j]
                            rate[face, e + a, j, pl.ds(pl.multiple_of(i * 8, 8), 8), :] = value

        def summed(face, x, j):
            value = rate[face, x, j]
            if x == 3:
                return value + rate[face, 4, j]
            if x == 4:
                return rate[face, 3, j] + value
            if x == 7:
                pair = jnp.where(low_half, rate[1 - face, 0, j], rate[face, 0, j])
                return value + pltpu.roll(pair, 64, 1)
            if x == 0:
                pair = jnp.where(low_half, rate[face, 7, j], rate[1 - face, 7, j])
                return value + pltpu.roll(pair, 64, 1)
            return value

        for face in range(2):
            for x in range(8):
                z = [summed(face, x, j) for j in range(4)]
                z[0], z[3] = (
                    z[0] + pltpu.roll(z[3], 1, 0),
                    z[3] + pltpu.roll(z[0], NODES - 1, 0),
                )
                for j in range(4):
                    rows = pl.ds(j, NODES, stride=4)
                    state[face, x, rows, :] = (
                        state[face, x, rows, :] + z[j] * inverse[face, x, rows, :]
                    )

    for face in range(2):
        for x in range(8):
            dyn[face, x * SIZE_Y : (x + 1) * SIZE_Y, :] = state[face, x, 0:SIZE_Y, :].astype(
                jnp.bfloat16
            )

    low_row = iota((2 * CHUNK, 128), 1) < 64

    @pl.loop(0, TILE_GROUPS)
    def _(i):
        @pl.when(i == TILE_GROUPS - 2)
        def _():
            arrived(forc_in.at[core], forc_recv.at[0])
            remote(
                forc_in.at[core],
                forc_in.at[core],
                forc_send.at[1],
                forc_recv.at[1],
                at(2 * chip + 1 - core),
            )

        chunks = [c for c, _, _ in chunks_of(i)]
        rows = [chunk_rows(c) for c in chunks]
        q = [
            [
                dot(
                    jnp.concatenate(
                        [place[face, r, xh * 1024 : (xh + 1) * 1024] for r in rows], axis=0
                    ),
                    dyn[face],
                )
                for xh in range(2)
            ]
            for face in range(2)
        ]
        turn = pltpu.roll(jnp.where(low_row, q[1][0], q[0][1]), 64, 1)
        packed = (jnp.where(low_row, q[0][0], q[1][1]) + turn).astype(jnp.bfloat16)
        for k in range(2):
            dyn_out[rows[k], :] = packed[k * CHUNK : (k + 1) * CHUNK, :]
        spread(i, chunks, dyn_out, dyn_in, dyn_recv.at[f * TILE_GROUPS + u_me])

    arrived(forc_in.at[1 - core], forc_recv.at[1])

    @pl.loop(0, COLUMNS // CHUNK // 2)
    def _(i):
        cols = pl.ds(pl.multiple_of(i * 2 * CHUNK, 2 * CHUNK), 2 * CHUNK)
        half = CHUNK
        blocks = []
        for k in range(0, half, per_peer):
            rows = pl.ds(pl.multiple_of(i * half + k, 16), per_peer)
            blocks += [forc_in[0, rows, :], forc_in[1, rows, :]]
        pre[:, cols] += dot(w_forc[...], jnp.concatenate(blocks, axis=0), NT)

    loads[6].wait()
    loads[7].wait()
    level_lane = iota((256, CHANNELS), 1)
    level_row = iota((256, CHANNELS), 0)

    @pl.loop(0, TILE_GROUPS)
    def _(i):
        steps = chunks_of(i)

        def arrive(u):
            for h in range(2):
                c = h * TILE_GROUPS + u
                arrived(dyn_in.at[chunk_rows(c)], dyn_recv.at[c])

        @pl.when(i != 2)
        def _():
            arrive(steps[0][2])

        @pl.when(i == 1)
        def _():
            arrive(steps[1][2])

        blocks, hidden = [], []
        for c, face, u in steps:
            halves = [dyn_in[chunk_rows(h * TILE_GROUPS + u), :] for h in range(2)]
            blocks.append(twice(*halves))
            first = w_dyn[:, pl.ds(pl.multiple_of(face * 256, 256), 256)]
            hidden.append(leaky(pre[:, chunk_rows(c)] + dot(first, blocks[-1].T)))
        hidden = twice(*hidden).astype(jnp.bfloat16)
        hidden = leaky(dot(w_mid_v[...], hidden) + twice(twice(bias_mid[...])))
        result = dot(w_out_v[...], hidden.astype(jnp.bfloat16)) + twice(twice(bias_out[...]))
        result = result.astype(jnp.bfloat16)
        for k, (c, face, u) in enumerate(steps):
            part = result[:, k * CHUNK : (k + 1) * CHUNK]
            diag_v[:, chunk_rows(c)] = part[CHANNELS:, :]
            row = level_lane // LEVELS * 16 + level_lane % 16
            row = row + level_lane // HALF % 2 * 128 + face * 64
            pick = (level_row == row).astype(jnp.bfloat16)
            change = part[0:CHANNELS, :].astype(jnp.float32).T
            value = dot(blocks[k], pick) + physics_weight * change
            back_out[chunk_rows(c), :] = value.astype(jnp.bfloat16)
        pair = [c for c, _, _ in steps]
        spread(i, pair, back_out, back_in, back_recv.at[f * TILE_GROUPS + u_me])

    diag_copy = pltpu.make_async_copy(diag_v, diagnostics, out_sem.at[0])
    diag_copy.start()

    updated_copies = []
    for v in (2, 1, 3, 0):
        u = lax.rem(u_me + TILE_GROUPS - v, TILE_GROUPS)
        parts = []
        for face in range(2):
            c = face * TILE_GROUPS + u
            rows = pl.ds(pl.multiple_of(c * CHUNK, CHUNK), CHUNK)
            arrived(back_in.at[rows], back_recv.at[c])
            parts.append((back_in[rows, :], rows))
        for k in range(0, COLUMNS, 512):
            value = sum(dot(back, place[f, rows, k : k + 512], TN) for back, rows in parts)
            value = value.astype(jnp.bfloat16)
            total[:, k : k + 512] = value if v == 2 else total[:, k : k + 512] + value
            if v == 0:
                cols = pl.ds(k, 512)
                updated_copies.append(
                    pltpu.make_async_copy(
                        total.at[:, cols], updated.at[:, cols], out_sem.at[1 + k // 512]
                    )
                )
                updated_copies[-1].start()
    for copy in sent:
        copy.wait_send()
    away = pl.ds(0, (devices - 1) * per_peer)
    for out in (dyn_out, back_out):
        arrived(out.at[away], relay_send)
    arrived(forc_out.at[pl.ds(0, (chips - 1) * per_peer)], forc_send.at[0])
    arrived(forc_in.at[core], forc_send.at[1])
    diag_copy.wait()
    for copy in updated_copies:
        copy.wait()


PIECES = 4


def finish(new, diag, updated, diagnostics, new_v, diag_v, updated_v, load_sem, out_sem):
    n, d = CHANNELS // PIECES, (OUT - CHANNELS) // PIECES // 16 * 16
    cuts = [pl.ds(k * n, n) for k in range(PIECES)]
    cuts += [pl.ds(k * d, d if k < PIECES - 1 else OUT - CHANNELS - k * d) for k in range(PIECES)]
    ends = ((new, new_v),) * PIECES + ((diag, diag_v),) * PIECES
    loads = [
        pltpu.make_async_copy(src.at[cut], dst.at[cut], load_sem.at[k])
        for k, (cut, (src, dst)) in enumerate(zip(cuts, ends))
    ]
    for copy in loads:
        copy.start()
    outs = []

    def out(src, dst):
        outs.append(pltpu.make_async_copy(src, dst, out_sem.at[len(outs)]))
        outs[-1].start()

    for k in range(PIECES):
        loads[k].wait()
        for x in range(SIZE_X):
            block = new_v[k * n : (k + 1) * n, x * SIZE_Y : (x + 1) * SIZE_Y]
            updated_v[pl.ds(k * n * SIZE_X + x, n, stride=SIZE_X), :] = block.astype(jnp.float32)
        rows = pl.ds(k * n * SIZE_X, n * SIZE_X)
        out(updated_v.at[rows], updated.at[rows])
    for k in range(PIECES, 2 * PIECES):
        loads[k].wait()
        out(diag_v.at[cuts[k]], diagnostics.at[cuts[k]])
    for copy in outs:
        copy.wait()


def local(
    tracers,
    wind_field,
    metric,
    forcing,
    aux_inputs,
    batch_pos,
    day_of_year,
    w_in,
    b_in,
    w_mid,
    b_mid,
    w_out,
    b_out,
):
    tiles = lax.axis_size("tile")
    anywhere = pl.BlockSpec(memory_space=pl.ANY)
    f32, b16 = jnp.float32, jnp.bfloat16
    dma = pltpu.SemaphoreType.DMA
    scratch = [
        pltpu.VMEM((CHANNELS * SIZE_X, SIZE_Y), f32),
        pltpu.VMEM((2 * LEVELS * SIZE_X, SIZE_Y), f32),
        pltpu.VMEM((SIZE_X, SIZE_Y), f32),
        pltpu.VMEM((12 * FORC, SIZE_X, SIZE_Y), b16),
        pltpu.VMEM((AUX, COLUMNS), b16),
        pltpu.VMEM(w_in.shape[::-1], b16),
        pltpu.VMEM(w_mid.shape, b16),
        pltpu.VMEM(w_out.shape, b16),
        pltpu.VMEM((SIZE_X, SIZE_Y), jnp.int32),
        pltpu.SMEM((1,), jnp.int32),
        pltpu.VMEM((HIDDEN,), f32),
        pltpu.VMEM((HIDDEN,), f32),
        pltpu.VMEM((OUT,), f32),
        dma((13,)),
        pltpu.VMEM((2, 8, SIZE_Y, 128), b16),
        pltpu.VMEM((2, 4, SIZE_Y, 128), b16),
        pltpu.VMEM((2, 8, SIZE_Y, 128), b16),
        pltpu.VMEM((2, 4, SIZE_Y, 128), b16),
        pltpu.VMEM((2, 2, 8, HALO, 128), b16),
        pltpu.VMEM((2, 2, 4, HALO, 128), b16),
        pltpu.VMEM((3, 2 * SIZE_X, SIZE_Y), f32),
        pltpu.VMEM((2, SIZE_X, SIZE_Y), jnp.int32),
        pltpu.VMEM((2, 8, WIDE, 128), f32),
        pltpu.VMEM((2, 2, 8, WIDE, 128), f32),
        pltpu.VMEM((2, 8, WIDE, 128), f32),
        pltpu.VMEM((2, 8, WIDE, 128), f32),
        pltpu.VMEM((2, 8, 4, NODES, 128), f32),
        pltpu.VMEM((2, COLUMNS, COLUMNS), b16),
        pltpu.VMEM((48 * SIZE_X, SIZE_Y), f32),
        pltpu.VMEM((128, COLUMNS), b16),
        pltpu.VMEM((COLUMNS // 2, 128), b16),
        pltpu.VMEM((2, COLUMNS // 2, 128), b16),
        pltpu.VMEM((2, COLUMNS // 2, 128), b16),
        pltpu.VMEM((COLUMNS, 128), b16),
        pltpu.VMEM((COLUMNS, 128), b16),
        pltpu.VMEM((COLUMNS, 128), b16),
        pltpu.VMEM((COLUMNS, 128), b16),
        pltpu.VMEM((HIDDEN, COLUMNS), f32),
        pltpu.VMEM((HIDDEN, AUX), b16),
        pltpu.VMEM((HIDDEN, 128), b16),
        pltpu.VMEM((HIDDEN, 512), b16),
        pltpu.VMEM((HIDDEN, 128), f32),
        pltpu.VMEM((HIDDEN, 128), f32),
        pltpu.VMEM((OUT, 128), f32),
        pltpu.VMEM((OUT - CHANNELS, COLUMNS), b16),
        pltpu.VMEM((CHANNELS, COLUMNS), b16),
        pltpu.SemaphoreType.REGULAR((2,)),
        dma((11,)),
        dma((11,)),
        dma((3, 2, 2)),
        dma((3, 2, 2)),
        dma,
        dma((2,)),
        dma((2,)),
        dma((2 * TILE_GROUPS,)),
        dma((2 * TILE_GROUPS,)),
        dma((5,)),
    ]
    updated, diagnostics = pl.pallas_call(
        functools.partial(kernel, tiles),
        out_shape=(
            jax.ShapeDtypeStruct((CHANNELS, COLUMNS), b16),
            jax.ShapeDtypeStruct((OUT - CHANNELS, COLUMNS), b16),
        ),
        in_specs=[anywhere] * 13,
        out_specs=(anywhere, anywhere),
        scratch_shapes=scratch,
        compiler_params=pltpu.CompilerParams(
            collective_id=0, has_side_effects=True, vmem_limit_bytes=60 * 2**20
        ),
    )(
        tracers.reshape(CHANNELS * SIZE_X, SIZE_Y),
        wind_field.reshape(2 * LEVELS * SIZE_X, SIZE_Y),
        metric,
        forcing.reshape(12 * FORC, SIZE_X, SIZE_Y),
        aux_inputs,
        batch_pos,
        day_of_year,
        w_in.T,
        b_in,
        w_mid,
        b_mid,
        w_out,
        b_out,
    )
    updated, diagnostics = pl.pallas_call(
        finish,
        out_shape=(
            jax.ShapeDtypeStruct((CHANNELS * SIZE_X, SIZE_Y), f32),
            jax.ShapeDtypeStruct((OUT - CHANNELS, COLUMNS), b16),
        ),
        in_specs=[anywhere, anywhere],
        out_specs=(anywhere, anywhere),
        scratch_shapes=[
            pltpu.VMEM((CHANNELS, COLUMNS), b16),
            pltpu.VMEM((OUT - CHANNELS, COLUMNS), b16),
            pltpu.VMEM((CHANNELS * SIZE_X, SIZE_Y), f32),
            dma((2 * PIECES,)),
            dma((2 * PIECES,)),
        ],
        compiler_params=pltpu.CompilerParams(vmem_limit_bytes=60 * 2**20),
    )(updated, diagnostics)
    return updated.reshape(tracers.shape), diagnostics


def solution(mesh):
    placed = (
        P(None, None, "face", "tile"),
        P(None, None, "face", "tile"),
        P("face", "tile"),
        P(None, None, "face", "tile"),
        P(None, ("face", "tile")),
        P("face", "tile"),
        P(),
        P(),
        P(),
        P(),
        P(),
        P(),
        P(),
    )
    return jax.shard_map(
        local,
        mesh=mesh,
        in_specs=placed,
        out_specs=(P(None, None, "face", "tile"), P(None, ("face", "tile"))),
        check_vma=False,
    )
```
